128 devices in a mesh: section: 2 (over y_hi), tensor: 2 (over core), dp: 32 (over z, x, y_lo).
Axes of the slice: x: 4, y: 4 (y_hi: 2, y_lo: 2; y = y_hi * 2 + y_lo), z: 4, core: 2. Of those that a mesh axis runs over, the one named last changes fastest.
Arguments:
- images: bfloat16 [32, 2, 1, 197, 1024], P('dp'), may hold values from -6 to 6
- cotangent: bfloat16 [32, 2, 1, 197, 1024], P('dp'), may hold values from -6 to 6
- shard_count: int32 [32], P('dp'), may hold values from 1 to 2, 48 in all
- slot_order: int32 [32, 2], P('dp'), may hold values from 0 to 1, each once within a row
- attend_gain: float32 [2, 1024], P('section'), may hold values from 0.5 to 1.5
- attend_input: bfloat16 [2, 1024, 3, 1024], P('section', None, None, 'tensor'), may hold values from -0.1875 to 0.1875
- attend_output: bfloat16 [2, 1024, 1024], P('section', 'tensor'), may hold values from -1.25 to 1.25
- feed_gain: float32 [2, 1024], P('section'), may hold values from 0.5 to 1.5
- feed_expand: bfloat16 [2, 1024, 4096], P('section', None, 'tensor'), may hold values from -0.1875 to 0.1875
- feed_reduce: bfloat16 [2, 4096, 1024], P('section', 'tensor'), may hold values from -0.09375 to 0.09375
Outputs:
- block_outputs: bfloat16 [2, 32, 2, 1, 197, 1024], P('section', 'dp')
- input_gradient: bfloat16 [2, 32, 2, 1, 197, 1024], P('section', 'dp')
- attend_gain_gradient: float32 [2, 1024], P('section', 'dp')
- attend_input_gradient: float32 [2, 1024, 3, 1024], P('section', 'dp', None, 'tensor')
- attend_output_gradient: float32 [2, 1024, 1024], P('section', ('tensor', 'dp'))
- feed_gain_gradient: float32 [2, 1024], P('section', 'dp')
- feed_expand_gradient: float32 [2, 1024, 4096], P('section', 'dp', 'tensor')
- feed_reduce_gradient: float32 [2, 4096, 1024], P('section', ('tensor', 'dp'))
The draws below stay inside these ranges and needn't reach their ends.
Inputs may be any that keep to these rules, and one draw needn't show every extreme that they name: `shard_count`: the counts sum to 48, and 16 shards hold 2 images. `slot_order`: each row is a permutation; its first shard_count entries name the slots that hold images.
All inputs are finite; a program needn't handle non-finite values.
Results may differ from the reference program's by a relative error of at most 0.03.
Values may be sent and summed in bfloat16 or wider, within the bound.
A program may use at most 128 MiB of HBM per device.

```python
import math
import jax
import jax.numpy as jnp
import numpy as np
from jax import lax

D = 1024
HEADS = 16
HEAD_DIM = 64
FF = 4096
LEN = 197
MICRO = 2
CAP = 1
IMAGES = 48
N_SECTION = 2
N_DP = 32


def shard_levels(stream_key, dims, cuts, least, high):
    level, own = 1.0, jax.random.fold_in(stream_key, 6)
    for position, shards_of in cuts:
        draws = jnp.exp(jax.random.uniform(jax.random.fold_in(own, position), (shards_of,), jnp.float32, least / len(cuts), high / len(cuts)))
        level = level * jnp.repeat(draws, dims[position] // shards_of).reshape([-1 if axis == position else 1 for axis in range(len(dims))])
    return level


def split_up(number_of, total, bound, slope):
    weights = [(1 << 20) // math.isqrt(standing ** slope) + 1 for standing in range(2, number_of + 1)]
    surplus, holding = total - bound - (number_of - 1), [1] * (number_of - 1)
    while surplus > 0:
        free = [i for i in range(number_of - 1) if holding[i] < bound]
        mass, left = sum([weights[i] for i in free]), surplus
        for i in free:
            more = min(bound - holding[i], max(1, left * weights[i] // mass), surplus)
            holding[i] = holding[i] + more
            surplus = surplus - more
    return np.array([bound] + holding)


def uneven(key, number_of, total, reach, slope):
    if number_of == 2:
        one = jax.random.randint(key, (), max(1, total - reach), min(reach, total - 1) + 1)
        return jnp.stack([one, total - one])
    tallies = jnp.asarray(split_up(number_of, total, reach, slope), jnp.int32)
    couples = (number_of - 1) // 2
    source_of, taker = tallies[1:1 + 2 * couples:2], tallies[2:2 + 2 * couples:2]
    margin = jnp.minimum(source_of - 1, reach - taker)
    shifted = jax.random.randint(jax.random.fold_in(key, 1), (couples,), 0, 1 << 20) % (margin + 1)
    tallies = tallies.at[1:1 + 2 * couples:2].set(source_of - shifted).at[2:2 + 2 * couples:2].set(taker + shifted)
    return tallies[jax.random.permutation(jax.random.fold_in(key, 2), number_of)]


def noise(own_key, extent, width, reach, cuts=(), kind=jnp.bfloat16):
    entries = jax.random.normal(own_key, extent, jnp.float32) * width
    if len(cuts) > 0:
        entries = shard_levels(own_key, extent, cuts, -0.22, 0.18) * entries
    return jnp.clip(entries, min=-reach, max=reach).astype(kind)


def setup_inputs(seed: int = 0) -> dict:
    streams_of = jax.random.split(jax.random.key(seed), 11)
    images = noise(streams_of[0], (N_DP, MICRO, CAP, LEN, D), 1.0, 6.0, ((0, 32),))
    cotangent = noise(streams_of[1], (N_DP, MICRO, CAP, LEN, D), 1.0, 6.0, ((0, 32),))
    shard_count = uneven(streams_of[2], N_DP, IMAGES, MICRO * CAP, 1).astype(jnp.int32)
    slot_order = jax.vmap(lambda own: jax.random.permutation(own, MICRO * CAP))(jax.random.split(streams_of[3], N_DP)).reshape((N_DP, MICRO * CAP)).astype(jnp.int32)
    attend_gain = jnp.clip(1.0 + 0.1 * jax.random.normal(streams_of[4], (N_SECTION, D), jnp.float32), 0.5, 1.5)
    attend_input = noise(streams_of[5], (N_SECTION, D, 3, D), D ** -0.5, 0.1875, ((0, 2), (3, 2)))
    attend_output = noise(streams_of[6], (N_SECTION, D, D), (max(4 * D // LEN, 1)) ** -0.5, 1.25, ((0, 2), (1, 2)))
    feed_gain = jnp.clip(1.0 + 0.1 * jax.random.normal(streams_of[7], (N_SECTION, D), jnp.float32), 0.5, 1.5)
    feed_expand = noise(streams_of[8], (N_SECTION, D, FF), D ** -0.5, 0.1875, ((0, 2), (2, 2)))
    feed_reduce = noise(streams_of[9], (N_SECTION, FF, D), FF ** -0.5, 0.09375, ((0, 2), (1, 2)))
    return dict(images=images, cotangent=cotangent, shard_count=shard_count, slot_order=slot_order, attend_gain=attend_gain, attend_input=attend_input, attend_output=attend_output, feed_gain=feed_gain, feed_expand=feed_expand, feed_reduce=feed_reduce)


@jax.custom_vjp
def low(v):
    return lax.optimization_barrier(v.astype(jnp.bfloat16)).astype(jnp.float32)

@jax.custom_vjp
def low_back(v):
    return v

def low_keep(v):
    return (low(v), None)

def low_pass(kept, grad):
    return (grad,)

def back_keep(v):
    return (v, None)

def back_low(kept, grad):
    return (low(grad),)
low.defvjp(low_keep, low_pass)
low_back.defvjp(back_keep, back_low)
highest = lax.Precision.HIGHEST
epsilon = 1e-06

def layer_norm(values, gain):
    centre = values - lax.optimization_barrier(jnp.mean(values, axis=-1, keepdims=True))
    scale_inv = lax.rsqrt(lax.optimization_barrier(jnp.mean(centre * centre, axis=-1, keepdims=True)) + epsilon)
    return centre * scale_inv * gain

def vision_block(residual, parameters):
    attend_gain, attend_input, attend_output, feed_gain, feed_expand, feed_reduce = parameters
    image_count, token_count, model_width = residual.shape
    norm_one = low(layer_norm(residual, attend_gain))
    projected = low_back(low(jnp.einsum('cld,dje->jcle', norm_one, attend_input, precision=highest)))
    split_heads = projected.reshape(3, image_count, token_count, HEADS, HEAD_DIM)
    scores = low_back(jnp.einsum('cqhe,ckhe->chqk', split_heads[0], split_heads[1], precision=highest) * 0.125)
    softmax_low = low(jax.nn.softmax(scores, axis=-1))
    mixed_heads = low_back(low(jnp.einsum('chqk,ckhe->cqhe', softmax_low, split_heads[2], precision=highest)))
    mixed_rows = mixed_heads.reshape(image_count, token_count, model_width)
    attend_sum = low_back(jnp.einsum('cle,ed->cld', mixed_rows, attend_output, precision=highest))
    middle = residual + attend_sum
    norm_two = low(layer_norm(middle, feed_gain))
    expanded = low_back(jnp.einsum('cld,df->clf', norm_two, feed_expand, precision=highest))
    activated = low(jax.nn.gelu(expanded, approximate=False))
    feed_sum = low_back(jnp.einsum('clf,fd->cld', activated, feed_reduce, precision=highest))
    return middle + feed_sum

def forward(first_input, handed_shift, parameters_one, parameters_two):
    entering = low_back(first_input)
    output_one = vision_block(entering, parameters_one)
    handed = low_back(low(output_one) + handed_shift)
    return (output_one, vision_block(handed, parameters_two))

def reference(images, cotangent, shard_count, slot_order, attend_gain, attend_input, attend_output, feed_gain, feed_expand, feed_reduce):
    slot_total = MICRO * CAP
    slot_numbers = jnp.arange(slot_total, dtype=jnp.int32)
    matches = slot_order[:, :, None] == slot_numbers[None, None, :]
    taken_rows = slot_numbers[None, :, None] < shard_count[:, None, None]
    live_slots = lax.optimization_barrier(jnp.sum(jnp.where(matches & taken_rows, 1.0, 0.0), axis=1)).astype(jnp.float32)
    section_parameters = [tuple((weight[section_index].astype(jnp.float32) for weight in (attend_gain, attend_input, attend_output, feed_gain, feed_expand, feed_reduce))) for section_index in range(2)]
    inputs = images.astype(jnp.float32).reshape(N_DP, slot_total, LEN, D)
    top_gradient = cotangent.astype(jnp.float32).reshape(N_DP, slot_total, LEN, D) * live_slots[:, :, None, None]

    def shard_step(totals, pieces):
        first_input, last_gradient = pieces
        handed_shift = jnp.zeros_like(first_input)
        results, pullback = jax.vjp(forward, first_input, handed_shift, section_parameters[0], section_parameters[1])
        first_gradient, handed_gradient, gradient_one, gradient_two = pullback((jnp.zeros_like(results[0]), last_gradient))
        totals = jax.tree.map(jnp.add, totals, (gradient_one, gradient_two))
        return (totals, (results[0], results[1], first_gradient, handed_gradient))
    zero_totals = jax.tree.map(jnp.zeros_like, (section_parameters[0], section_parameters[1]))
    totals, (output_one, output_two, first_gradient, handed_gradient) = lax.scan(shard_step, zero_totals, (inputs, top_gradient))
    full_shape = (N_DP, MICRO, CAP, LEN, D)
    block_outputs = jnp.stack([output_one.reshape(full_shape), output_two.reshape(full_shape)]).astype(jnp.bfloat16)
    input_gradient = jnp.stack([first_gradient.reshape(full_shape), handed_gradient.reshape(full_shape)]).astype(jnp.bfloat16)
    stacked = [jnp.stack([first_part, second_part]) for first_part, second_part in zip(totals[0], totals[1])]
    return (block_outputs, input_gradient, stacked[0], stacked[1], stacked[2], stacked[3], stacked[4], stacked[5])
```

```python
import functools

import jax
import jax.numpy as jnp
from jax import lax
from jax.experimental import pallas as pl
from jax.experimental.pallas import tpu as pltpu
from jax.sharding import PartitionSpec as P

f32 = jnp.float32
bf16 = jnp.bfloat16
MESH = pl.DeviceIdType.MESH

TOKENS = 197
PAD = 208
IMGS = 2
ROWS = IMGS * PAD
D = 1024
WIDE = 2048
HALF = 512
QKV = 3 * HALF
ROW_CHUNK = 32
N_CHUNK = ROWS // ROW_CHUNK
EPS = 1e-06

GRADS = ((64, D), (32, WIDE), (16, D), (32, QKV), (16, 256))


def _streams():
    groups = []

    def pair(m, r0, r, c0, c):
        groups.append(((m, r0, r, c0, c // 2, 0), (m, r0, r, c0 + c // 2, c // 2, 1)))

    pair(0, 0, 32, 0, 1024)
    pair(0, 32, 32, 0, 1024)
    pair(1, 0, 32, 0, 1024)
    pair(1, 0, 32, 1024, 1024)
    pair(2, 0, 16, 0, 1024)
    pair(3, 0, 32, 1024, 512)
    pair(3, 0, 32, 0, 512)
    pair(3, 0, 32, 512, 512)
    groups.append(((4, 0, 16, 0, 256, 0),))
    return groups


GROUPS = _streams()
STREAMS = [s for g in GROUPS for s in g]
BUF_NAMES = ("b1", "b2", "b3", "c1", "c2")


def _buffers(spec):
    r, h = spec[2], spec[4] // 2
    return (
        (2, 4, 2, r, h),
        (2, 2, 4, 2, r, h),
        (2, 4, r, h),
        (2, r, h),
        (2, 2, r, h),
    )


def _loop(n, body):
    def step(i, c):
        body(i)
        return c

    lax.fori_loop(0, n, step, 0)


def _add_into(dst, srcs):
    if len(dst.shape) == 2:
        v = srcs[0][...].astype(f32)
        for s in srcs[1:]:
            v = v + s[...].astype(f32)
        dst[...] = v.astype(dst.dtype)
        return

    def body(i):
        v = srcs[0][i].astype(f32)
        for s in srcs[1:]:
            v = v + s[i].astype(f32)
        dst[i] = v.astype(dst.dtype)

    _loop(dst.shape[0], body)


class _Stream:
    def __init__(self, index, spec, grads, bufs, outs, sems, coords):
        self.index, self.spec, self.grads, self.b, self.outs = index, spec, grads, bufs, outs
        self.send_sem, self.recv_sem = sems
        self.H = self.b["b2"].at[0]
        self.K = self.b["b3"]
        self.co = coords

    def g(self, j, half):
        m, r0, r, c0, c, order = self.spec
        h = c // 2
        grad = self.grads[m]
        rows, cols = pl.ds(r0, r), pl.ds(c0 + half * h, h)
        return grad.at[j, :, :, rows, cols] if order == 0 else grad.at[:, j, :, rows, cols]

    def kk(self, j, half):
        return self.K.at[half, j]

    def peer(self, axis, d):
        z, x, y = self.co
        if axis == "y":
            y = 1 - y
        elif axis == "z":
            z = lax.rem(z + d + 4, 4)
        else:
            x = lax.rem(x + d + 4, 4)
        return {"dp": z * 8 + x * 2 + y}

    def copy(self, k, src, dst, axis, d):
        return pltpu.make_async_remote_copy(
            src_ref=src,
            dst_ref=dst,
            send_sem=self.send_sem.at[self.index, k],
            recv_sem=self.recv_sem.at[self.index, k],
            device_id=self.peer(axis, d),
            device_id_type=MESH,
        )

    def ring(self, phase):
        axis = ("zx", "xz")[self.spec[5]][phase]
        p = self.co[0] if axis == "z" else self.co[1]
        src = (self.g, self.kk)[phase]
        one, two = (self.b["b1"], self.b["b2"]) if phase == 0 else (self.b["c1"], self.b["c2"])
        return axis, (lambda d: lax.rem(p + d + 4, 4)), src, one, two, 7 * phase

    def ring_copy(self, phase, n):
        axis, at, src, one, two, k = self.ring(phase)
        source, dst, step = (
            (lambda: src(at(2), 0), one.at[0], 1),
            (lambda: src(at(2), 1), one.at[1], -1),
            (lambda: src(at(1), 1), two.at[0, 1], 1),
            (lambda: src(at(-1), 0), two.at[1, 0], -1),
            (lambda: one.at[0], two.at[0, 0], 1),
            (lambda: one.at[1], two.at[1, 1], -1),
        )[n]
        return self.copy(k + n, source(), dst, axis, step)

    def ring_start(self, phase):
        for n in range(4):
            self.ring_copy(phase, n).start()

    def ring_mid(self, phase):
        axis, at, src, one, two, k = self.ring(phase)
        self.ring_copy(phase, 0).wait_recv()
        _add_into(one.at[0], [one.at[0], src(at(1), 0)])
        self.ring_copy(phase, 4).start()
        self.ring_copy(phase, 1).wait_recv()
        _add_into(one.at[1], [one.at[1], src(at(-1), 1)])
        self.ring_copy(phase, 5).start()

    def ring_end(self, phase):
        for n in range(2, 6):
            self.ring_copy(phase, n).wait_recv()

    def y_copy(self):
        return self.copy(6, self.H.at[:, :, 1 - self.co[2]], self.b["b3"], "y", 0)

    def stage(self, n):
        getattr(self, "stage%d" % n)()

    def stage0(self):
        self.ring_start(0)

    def stage1(self):
        self.ring_mid(0)

    def stage2(self):
        self.ring_end(0)
        p = self.ring(0)[1](0)
        two = self.b["b2"]
        for half in (0, 1):
            _add_into(self.H.at[half], [self.g(p, half), two.at[0, half], two.at[1, half]])
        self.y_copy().start()

    def stage3(self):
        self.y_copy().wait_recv()
        for half in (0, 1):
            _add_into(
                self.K.at[half],
                [self.H.at[half, :, self.co[2]], self.b["b3"].at[half]],
            )
        self.ring_start(1)

    def stage4(self):
        self.ring_mid(1)

    def stage5(self):
        self.ring_end(1)
        p = self.ring(1)[1](0)
        two = self.b["c2"]
        m, r0, r, c0, c, order = self.spec
        h = c // 2
        for half in (0, 1):
            v = self.K[half, p].astype(f32) + two[0, half].astype(f32)
            self.outs[m][pl.ds(r0, r), pl.ds(c0 + half * h, h)] = v + two[1, half].astype(f32)

    def drain(self):
        for phase in (0, 1):
            for n in range(6):
                self.ring_copy(phase, n).wait_send()
        self.y_copy().wait_send()


def _nn(a, b):
    return lax.dot_general(a, b, (((1,), (0,)), ((), ())), preferred_element_type=f32)


def _nt(a, b):
    return lax.dot_general(a, b, (((1,), (1,)), ((), ())), preferred_element_type=f32)


def _tn(a, b):
    return lax.dot_general(a, b, (((0,), (0,)), ((), ())), preferred_element_type=f32)


def _norm(v):
    centre = v - jnp.mean(v, axis=-1, keepdims=True)
    inv = lax.rsqrt(jnp.mean(centre * centre, axis=-1, keepdims=True) + EPS)
    return centre * inv, inv


def _norm_back(upstream, hat, inv, gain):
    q = upstream * gain
    return inv * (
        q - jnp.mean(q, axis=-1, keepdims=True) - hat * jnp.mean(q * hat, axis=-1, keepdims=True)
    )


def _cols(i, n):
    return pl.ds(pl.multiple_of(i * n, n), n)


def _kernel(*refs):
    (images, cotangent, gain_one, gain_two, wqkv_in, wo_in, w1_in, w2_in) = refs[:8]
    (y_ref, ig_ref, o_w2, o_w1, o_wo, o_qkv, o_gain) = refs[8:15]
    rest = refs[15:]
    (
        wqkv, wo, w1, w2, g_w2, g_w1, g_wo, g_qkv, g_gain,
        xb, eb, hin, n1, pr, pb, mx, mid, n2, act, gp, eg, mlow, pg, sendb, recvb, gacc,
        load_sem, x_ss, x_rs, hop_sem, rs_ss, rs_rs,
    ) = rest[:32]
    ring_bufs = rest[32:]

    section = lax.axis_index("section")
    tensor = lax.axis_index("tensor")
    dp = lax.axis_index("dp")
    z, x, y = dp // 8, lax.rem(dp // 2, 4), lax.rem(dp, 2)

    loads = [
        pltpu.make_async_copy(src, dst, load_sem.at[i])
        for i, (src, dst) in enumerate(
            ((images, xb), (wqkv_in, wqkv), (wo_in, wo), (w1_in, w1), (w2_in, w2), (cotangent, eb))
        )
    ]
    for c in loads:
        c.start()

    barrier = pltpu.get_barrier_semaphore()

    def r4(v):
        return lax.rem(v + 4, 4)

    for peer in (
        {"tensor": 1 - tensor},
        {"section": 1 - section},
        {"dp": r4(z + 1) * 8 + x * 2 + y},
        {"dp": r4(z - 1) * 8 + x * 2 + y},
        {"dp": z * 8 + r4(x + 1) * 2 + y},
        {"dp": z * 8 + r4(x - 1) * 2 + y},
        {"dp": z * 8 + x * 2 + 1 - y},
    ):
        pl.semaphore_signal(barrier, inc=1, device_id=peer, device_id_type=MESH)
    pl.semaphore_wait(barrier, 7)

    def exchange(par, chunk):
        part = (slice(None), pl.ds(chunk * 512, 512))
        return pltpu.make_async_remote_copy(
            src_ref=sendb.at[par].at[part],
            dst_ref=recvb.at[par].at[part],
            send_sem=x_ss.at[par, chunk],
            recv_sem=x_rs.at[par, chunk],
            device_id={"tensor": 1 - tensor},
            device_id_type=MESH,
        )

    def exchange_wait(par):
        for chunk in (0, 1):
            exchange(par, chunk).wait()

    own_half = pl.ds(pl.multiple_of(tensor * 512, 512), 512)
    other_half = pl.ds(pl.multiple_of((1 - tensor) * 512, 512), 512)

    def hop(src):
        return pltpu.make_async_remote_copy(
            src_ref=src.at[:, own_half],
            dst_ref=hin.at[:, own_half],
            send_sem=hop_sem.at[0],
            recv_sem=hop_sem.at[1],
            device_id={"section": 1 - section},
            device_id_type=MESH,
        )

    def forward_half(cols):
        return pltpu.make_async_remote_copy(
            src_ref=hin.at[:, cols],
            dst_ref=hin.at[:, cols],
            send_sem=hop_sem.at[2],
            recv_sem=hop_sem.at[3],
            device_id={"tensor": 1 - tensor},
            device_id_type=MESH,
        )

    def receive(src, dst):
        hop(src).wait_recv()
        forward_half(own_half).start()
        forward_half(own_half).wait_send()
        forward_half(other_half).wait_recv()

        def body(i):
            rows = _cols(i, ROW_CHUNK)
            dst[rows, :] = hin[rows, :]

        _loop(N_CHUNK, body)

    lane = lax.broadcasted_iota(jnp.int32, (1, 128), 1)
    head_masks = ((lane < 64).astype(bf16), (lane >= 64).astype(bf16))
    key_ok = lax.broadcasted_iota(jnp.int32, (PAD, PAD), 1) < TOKENS

    def forward(tick):
        @pl.when(jnp.logical_and(tick == 1, section == 1))
        def _():
            receive(y_ref, xb)

        def ln_one(i):
            rows = _cols(i, ROW_CHUNK)
            hat, inv = _norm(xb[rows, :].astype(f32))
            n1[rows, :] = (hat * gain_one[...]).astype(bf16)

        _loop(N_CHUNK, ln_one)

        @pl.when(tick == 0)
        def _():
            loads[1].wait()

        def project(i):
            pr[:, _cols(i, 512)] = _nn(n1[...], wqkv[:, _cols(i, 512)]).astype(bf16)

        _loop(3, project)

        def attend(i):
            img, pair_i = i // 4, lax.rem(i, 4)
            rows = _cols(img, PAD)
            q = pr[rows, _cols(pair_i, 128)]
            k = pr[rows, _cols(pair_i + 4, 128)]
            v = pr[rows, _cols(pair_i + 8, 128)]
            total = None
            for h in (0, 1):
                s = _nt(q * head_masks[h], k) * 0.125
                s = jnp.where(key_ok, s, -1e30)
                e = jnp.exp(s - jnp.max(s, axis=-1, keepdims=True))
                p = (e / jnp.sum(e, axis=-1, keepdims=True)).astype(bf16)
                pb[i * 2 + h] = p
                t = _nn(p, v * head_masks[h])
                total = t if total is None else total + t
            mx[rows, _cols(pair_i, 128)] = total.astype(bf16)

        _loop(8, attend)

        @pl.when(tick == 0)
        def _():
            loads[2].wait()

        for chunk in (0, 1):
            part = pl.ds(chunk * 512, 512)
            sendb[0, :, part] = _nn(mx[...], wo[:, part]).astype(bf16)
            exchange(0, chunk).start()
        exchange_wait(0)

        def ln_two(i):
            rows = _cols(i, ROW_CHUNK)
            m = xb[rows, :].astype(f32) + (
                sendb[0, rows, :].astype(f32) + recvb[0, rows, :].astype(f32)
            )
            mid[rows, :] = m
            hat, inv = _norm(m)
            n2[rows, :] = (hat * gain_two[...]).astype(bf16)

        _loop(N_CHUNK, ln_two)

        @pl.when(tick == 0)
        def _():
            loads[3].wait()

        def expand(i):
            part = _cols(i, 256)
            e = _nn(n2[...], w1[:, part])
            phi = 0.5 * (1.0 + lax.erf(e * 0.7071067811865476))
            act[:, part] = (e * phi).astype(bf16)
            gp[:, part] = (phi + e * (jnp.exp(-0.5 * e * e) * 0.3989422804014327)).astype(bf16)

        _loop(8, expand)

        @pl.when(tick == 0)
        def _():
            loads[4].wait()

        for chunk in (0, 1):
            part = pl.ds(chunk * 512, 512)
            sendb[1, :, part] = _nn(act[...], w2[:, part]).astype(bf16)
            exchange(1, chunk).start()
        exchange_wait(1)

        def finish(i):
            rows = _cols(i, ROW_CHUNK)
            v = mid[rows, :] + (sendb[1, rows, :].astype(f32) + recvb[1, rows, :].astype(f32))
            y_ref[rows, :] = v.astype(bf16)

        _loop(N_CHUNK, finish)

        @pl.when(jnp.logical_and(tick == 0, section == 0))
        def _():
            hop(y_ref).start()
            hop(y_ref).wait_send()

    loads[0].wait()
    _loop(2, forward)
    loads[5].wait()

    grads = (g_w2, g_w1, g_wo, g_qkv, g_gain)
    outs = (o_w2, o_w1, o_wo, o_qkv, o_gain)
    nb = len(BUF_NAMES)
    streams = [
        _Stream(
            i, spec, grads, dict(zip(BUF_NAMES, ring_bufs[i * nb : (i + 1) * nb])), outs,
            (rs_ss, rs_rs), (z, x, y),
        )
        for i, spec in enumerate(STREAMS)
    ]
    groups, count = [], 0
    for g in GROUPS:
        groups.append(streams[count : count + len(g)])
        count += len(g)

    def start_group(i):
        for s in groups[i]:
            s.stage(0)

    def pump(tick):
        for st in (1, 2, 3, 4, 5):
            i = tick - st
            if 0 <= i < len(groups):
                for s in groups[i]:
                    s.stage(st)

    def pack_gain(row, half):
        lanes = lax.broadcasted_iota(jnp.int32, (1024, 128), 0)
        pick = (lax.rem(lanes, 32) == lax.broadcasted_iota(jnp.int32, (1024, 128), 1)).astype(bf16)
        for zz in range(4):
            r = lax.broadcasted_iota(jnp.int32, (128, 1024), 0) // 16 + zz * 8
            c = lax.broadcasted_iota(jnp.int32, (128, 1024), 1) // 32
            spread = jnp.where(r == c, row, 0.0).astype(bf16)
            g_gain[zz, :, :, :, pl.ds(half * 128, 128)] = (
                _nn(spread, pick).astype(bf16).reshape(4, 2, 16, 128)
            )

    def backward(tick):
        last = tick == 1

        @pl.when(jnp.logical_and(last, section == 0))
        def _():
            receive(ig_ref, eb)

        @pl.when(last)
        def _():
            def tile(i):
                for n in (0, 1):
                    part = pl.ds(n * 512, 512)
                    t = _tn(act[:, _cols(i, 256)], eb[:, part]).astype(bf16)
                    g_w2[i // 2, pl.ds(lax.rem(i, 2) * 2, 2), :, :, part] = t.reshape(2, 2, 64, 512)

            _loop(8, tile)
            start_group(0)
            start_group(1)

        def expand_back(i):
            part = _cols(i, 256)
            d = _nt(eb[...], w2[part, :])
            eg[:, part] = (d * gp[:, part].astype(f32)).astype(bf16)

        _loop(8, expand_back)

        @pl.when(last)
        def _():
            pump(1)

        for chunk in (0, 1):
            part = pl.ds(chunk * 512, 512)
            sendb[0, :, part] = _nt(eg[...], w1[part, :]).astype(bf16)
            exchange(0, chunk).start()

        @pl.when(last)
        def _():
            def tile(i):
                for n in range(4):
                    part = pl.ds(n * 512, 512)
                    t = _tn(n2[:, _cols(i, 256)], eg[:, part]).astype(bf16)
                    g_w1[i, :, :, :, part] = t.reshape(4, 2, 32, 512)

            _loop(4, tile)
            start_group(2)
            start_group(3)

        exchange_wait(0)
        gacc[...] = jnp.zeros_like(gacc)

        def ln_two_back(i):
            rows = _cols(i, ROW_CHUNK)
            dn = sendb[0, rows, :].astype(f32) + recvb[0, rows, :].astype(f32)
            hat, inv = _norm(mid[rows, :])
            gacc[0:1, :] += jnp.sum(dn * hat, axis=0, keepdims=True)
            m = eb[rows, :].astype(f32) + _norm_back(dn, hat, inv, gain_two[...])
            mlow[rows, :] = m.astype(bf16)

        _loop(N_CHUNK, ln_two_back)

        sendb[1, :, pl.ds(0, HALF)] = _nt(mlow[...], wo[...]).astype(bf16)

        @pl.when(last)
        def _():
            pump(2)

            def tile(i):
                for n in (0, 1):
                    part = pl.ds(n * 512, 512)
                    t = _tn(mx[:, _cols(i, 256)], mlow[:, part]).astype(bf16)
                    g_wo[pl.ds(i * 2, 2), :, :, :, part] = t.reshape(2, 4, 2, 16, 512)

            _loop(2, tile)
            start_group(4)
            pump(3)

        def attend_back(i):
            img, pair_i = i // 4, lax.rem(i, 4)
            rows = _cols(img, PAD)
            q = pr[rows, _cols(pair_i, 128)]
            k = pr[rows, _cols(pair_i + 4, 128)]
            v = pr[rows, _cols(pair_i + 8, 128)]
            do = sendb[1, rows, _cols(pair_i, 128)]
            sums = [None, None, None]
            for h in (0, 1):
                mask = head_masks[h]
                p = pb[i * 2 + h]
                pf = p.astype(f32)
                doh = do * mask
                dpr = _nt(doh, v)
                inner = jnp.sum(dpr * pf, axis=-1, keepdims=True)
                ds = (pf * (dpr - inner)).astype(bf16)
                for j, t in enumerate((_nn(ds, k * mask), _tn(ds, q * mask), _tn(p, doh))):
                    sums[j] = t if sums[j] is None else sums[j] + t
            for j, scale in enumerate((0.125, 0.125, 1.0)):
                pg[rows, _cols(pair_i + 4 * j, 128)] = (sums[j] * scale).astype(bf16)

        _loop(8, attend_back)

        @pl.when(last)
        def _():
            pump(4)

        for chunk in (0, 1):
            part = pl.ds(chunk * 512, 512)
            sendb[1, :, part] = _nt(pg[...], wqkv[part, :]).astype(bf16)
            exchange(1, chunk).start()

        @pl.when(last)
        def _():
            def tile(i):
                for n in range(3):
                    part = pl.ds(n * 512, 512)
                    t = _tn(n1[:, _cols(i, 256)], pg[:, part]).astype(bf16)
                    g_qkv[i, :, :, :, part] = t.reshape(4, 2, 32, 512)

            _loop(4, tile)
            for i in (5, 6, 7):
                start_group(i)

        exchange_wait(1)

        def ln_one_back(i):
            rows = _cols(i, ROW_CHUNK)
            dn = sendb[1, rows, :].astype(f32) + recvb[1, rows, :].astype(f32)
            hat, inv = _norm(xb[rows, :].astype(f32))
            gacc[1:2, :] += jnp.sum(dn * hat, axis=0, keepdims=True)
            m = mlow[rows, :].astype(f32) + _norm_back(dn, hat, inv, gain_one[...])
            ig_ref[rows, :] = m.astype(bf16)

        _loop(N_CHUNK, ln_one_back)

        @pl.when(jnp.logical_and(tick == 0, section == 1))
        def _():
            hop(ig_ref).start()
            hop(ig_ref).wait_send()

    _loop(2, backward)
    pack_gain(gacc[1:2, :], 0)
    pack_gain(gacc[0:1, :], 1)
    start_group(8)
    for tick in range(5, len(groups) + 5):
        pump(tick)
    for s in streams:
        s.drain()


def _call(*args):
    vmem = pl.BlockSpec(memory_space=pltpu.VMEM)
    hbm = pl.BlockSpec(memory_space=pl.ANY)
    out_shape = [jax.ShapeDtypeStruct((ROWS, D), bf16)] * 2 + [
        jax.ShapeDtypeStruct(s, f32) for s in GRADS
    ]
    scratch = [
        pltpu.VMEM((D, QKV), bf16),
        pltpu.VMEM((HALF, D), bf16),
        pltpu.VMEM((D, WIDE), bf16),
        pltpu.VMEM((WIDE, D), bf16),
    ]
    scratch += [pltpu.VMEM((4, 4, 2) + s, bf16) for s in GRADS]
    scratch += [
        pltpu.VMEM((ROWS, D), bf16),
        pltpu.VMEM((ROWS, D), bf16),
        pltpu.VMEM((ROWS, D), bf16),
        pltpu.VMEM((ROWS, D), bf16),
        pltpu.VMEM((ROWS, QKV), bf16),
        pltpu.VMEM((16, PAD, PAD), bf16),
        pltpu.VMEM((ROWS, HALF), bf16),
        pltpu.VMEM((ROWS, D), f32),
        pltpu.VMEM((ROWS, D), bf16),
        pltpu.VMEM((ROWS, WIDE), bf16),
        pltpu.VMEM((ROWS, WIDE), bf16),
        pltpu.VMEM((ROWS, WIDE), bf16),
        pltpu.VMEM((ROWS, D), bf16),
        pltpu.VMEM((ROWS, QKV), bf16),
        pltpu.VMEM((2, ROWS, D), bf16),
        pltpu.VMEM((2, ROWS, D), bf16),
        pltpu.VMEM((8, D), f32),
        pltpu.SemaphoreType.DMA((6,)),
        pltpu.SemaphoreType.DMA((2, 2)),
        pltpu.SemaphoreType.DMA((2, 2)),
        pltpu.SemaphoreType.DMA((4,)),
        pltpu.SemaphoreType.DMA((len(STREAMS), 13)),
        pltpu.SemaphoreType.DMA((len(STREAMS), 13)),
    ]
    for s in STREAMS:
        scratch += [pltpu.VMEM(b, bf16) for b in _buffers(s)]
    return pl.pallas_call(
        _kernel,
        out_shape=out_shape,
        in_specs=[hbm, hbm, vmem, vmem, hbm, hbm, hbm, hbm],
        out_specs=[vmem] * len(out_shape),
        scratch_shapes=scratch,
        compiler_params=pltpu.CompilerParams(
            collective_id=0, has_side_effects=True, vmem_limit_bytes=63 << 20
        ),
    )(*args)


def per_device(
    images, cotangent, shard_count, slot_order, attend_gain, attend_input, attend_output,
    feed_gain, feed_expand, feed_reduce,
):
    slots = jnp.arange(IMGS, dtype=jnp.int32)
    matches = slot_order[0][:, None] == slots[None, :]
    taken = (slots < shard_count[0])[:, None]
    live = jnp.any(matches & taken, axis=0).astype(bf16)

    def padded(v):
        return jnp.pad(v, ((0, 0), (0, PAD - TOKENS), (0, 0))).reshape(ROWS, D)

    top = cotangent[0, :, 0] * live[:, None, None]
    y, ig, d_w2, d_w1, d_wo, d_qkv, d_gain = _call(
        padded(images[0, :, 0]), padded(top), attend_gain, feed_gain,
        attend_input[0].reshape(D, QKV), attend_output[0], feed_expand[0], feed_reduce[0],
    )

    def cut(v):
        return v.reshape(IMGS, PAD, D)[:, :TOKENS].reshape(1, 1, IMGS, 1, TOKENS, D)

    return (
        cut(y), cut(ig), d_gain[0:1, 0:32], d_qkv.reshape(1, 32, 3, HALF), d_wo[None],
        d_gain[0:1, 128:160], d_w1[None], d_w2[None],
    )


def solution(mesh):
    in_specs = (
        P("dp", None, None, None, None),
        P("dp", None, None, None, None),
        P("dp"),
        P("dp", None),
        P("section", None),
        P("section", None, None, "tensor"),
        P("section", "tensor", None),
        P("section", None),
        P("section", None, "tensor"),
        P("section", "tensor", None),
    )
    out_specs = (
        P("section", "dp", None, None, None, None),
        P("section", "dp", None, None, None, None),
        P("section", "dp"),
        P("section", "dp", None, "tensor"),
        P("section", ("tensor", "dp"), None),
        P("section", "dp"),
        P("section", "dp", "tensor"),
        P("section", ("tensor", "dp"), None),
    )
    return jax.shard_map(
        per_device, mesh=mesh, in_specs=in_specs, out_specs=out_specs, check_vma=False
    )
```

```python
import functools

import jax
import jax.numpy as jnp
from jax import lax
from jax.experimental import pallas as pl
from jax.experimental.pallas import tpu as pltpu
from jax.sharding import PartitionSpec as P

f32 = jnp.float32
bf16 = jnp.bfloat16
MESH = pl.DeviceIdType.MESH

TOKENS = 197
PAD = 208
IMGS = 2
ROWS = IMGS * PAD
D = 1024
WIDE = 2048
HALF = 512
QKV = 3 * HALF
ROW_CHUNK = 32
N_CHUNK = ROWS // ROW_CHUNK
EPS = 1e-06

GRADS = ((64, D), (32, WIDE), (16, D), (32, QKV), (16, 256))


def _streams():
    groups = []

    def pair(m, r0, r, c0, c, order=0):
        groups.append(((m, r0, r, c0, c // 2, order), (m, r0, r, c0 + c // 2, c // 2, order + 1)))

    pair(0, 0, 32, 0, 1024)
    pair(0, 32, 32, 0, 1024, 2)
    pair(1, 0, 32, 0, 1024)
    pair(1, 0, 32, 1024, 1024)
    pair(2, 0, 16, 0, 1024)
    pair(3, 0, 32, 1024, 512)
    pair(3, 0, 32, 0, 512)
    pair(3, 0, 32, 512, 512)
    groups.append(((4, 0, 16, 0, 256, 0),))
    return groups


GROUPS = _streams()
STEPS = {
    "eb0": (),
    "W2": ((0, 0), (1, 0)),
    "eb1": (),
    "et": ((0, 1),),
    "W1": ((2, 0), (3, 0)),
    "ln2": ((0, 2),),
    "Wo": ((4, 0),),
    "at0": ((2, 1),),
    "at1": (),
    "it": ((3, 1),),
    "QKV": ((4, 1), (5, 0)),
    "ln1": ((1, 1),),
    "gain": (),
    "tail": ((6, 0), (2, 2), (7, 0), (0, 3), (3, 2), (4, 2), (5, 1), (8, 0), (2, 3), (1, 2), (6, 1), (3, 3), (7, 1), (0, 4), (4, 3), (5, 2), (8, 1), (2, 4), (1, 3), (6, 2), (3, 4), (5, 3), (7, 2), (0, 5), (4, 4), (8, 2), (2, 5), (1, 4), (3, 5), (5, 4), (6, 3), (4, 5), (1, 5), (5, 5), (6, 4), (7, 3), (8, 3), (6, 5), (7, 4), (8, 4), (7, 5), (8, 5)),
}
STREAMS = [s for g in GROUPS for s in g]
BUF_NAMES = ("b1", "b2", "b3", "c1", "c2")


def _buffers(spec):
    r, h = spec[2], spec[4] // 2
    if spec[5] >= 2:
        return ((2, 4, r, h), (2, 2, 4, r, h), (4, 4, r, 2 * h), (2, r, h), (2, 2, r, h))
    return (
        (2, 4, 2, r, h),
        (2, 2, 4, 2, r, h),
        (2, 4, r, h),
        (2, r, h),
        (2, 2, r, h),
    )


def _loop(n, body):
    def step(i, c):
        body(i)
        return c

    lax.fori_loop(0, n, step, 0)


def _add_into(dst, srcs):
    if len(dst.shape) == 2:
        v = srcs[0][...].astype(f32)
        for s in srcs[1:]:
            v = v + s[...].astype(f32)
        dst[...] = v.astype(dst.dtype)
        return

    def body(i):
        v = srcs[0][i].astype(f32)
        for s in srcs[1:]:
            v = v + s[i].astype(f32)
        dst[i] = v.astype(dst.dtype)

    _loop(dst.shape[0], body)


class _Stream:
    def __init__(self, index, spec, grads, bufs, outs, sems, coords):
        self.index, self.spec, self.grads, self.b, self.outs = index, spec, grads, bufs, outs
        self.send_sem, self.recv_sem = sems
        self.H = self.b["b2"].at[0]
        self.K = self.b["b3"]
        self.y_first = spec[5] >= 2
        self.co = coords

    def g(self, j, half):
        m, r0, r, c0, c, order = self.spec
        h = c // 2
        grad = self.grads[m]
        rows, cols = pl.ds(r0, r), pl.ds(c0 + half * h, h)
        if self.y_first:
            cols = pl.ds(half * h, h)
            return self.K.at[j, :, :, cols] if order == 2 else self.K.at[:, j, :, cols]
        return grad.at[j, :, :, rows, cols] if order == 0 else grad.at[:, j, :, rows, cols]

    def kk(self, j, half):
        return self.H.at[half, j] if self.y_first else self.K.at[half, j]

    def peer(self, axis, d):
        z, x, y = self.co
        if axis == "y":
            y = 1 - y
        elif axis == "z":
            z = lax.rem(z + d + 4, 4)
        else:
            x = lax.rem(x + d + 4, 4)
        return {"dp": z * 8 + x * 2 + y}

    def copy(self, k, src, dst, axis, d):
        return pltpu.make_async_remote_copy(
            src_ref=src,
            dst_ref=dst,
            send_sem=self.send_sem.at[self.index, k],
            recv_sem=self.recv_sem.at[self.index, k],
            device_id=self.peer(axis, d),
            device_id_type=MESH,
        )

    def ring(self, phase):
        axis = ("zx", "xz")[self.spec[5] % 2][phase]
        p = self.co[0] if axis == "z" else self.co[1]
        src = (self.g, self.kk)[phase]
        one, two = (self.b["b1"], self.b["b2"]) if phase == 0 else (self.b["c1"], self.b["c2"])
        return axis, (lambda d: lax.rem(p + d + 4, 4)), src, one, two, 7 * phase

    def ring_copy(self, phase, n):
        axis, at, src, one, two, k = self.ring(phase)
        source, dst, step = (
            (lambda: src(at(2), 0), one.at[0], 1),
            (lambda: src(at(2), 1), one.at[1], -1),
            (lambda: src(at(1), 1), two.at[0, 1], 1),
            (lambda: src(at(-1), 0), two.at[1, 0], -1),
            (lambda: one.at[0], two.at[0, 0], 1),
            (lambda: one.at[1], two.at[1, 1], -1),
        )[n]
        return self.copy(k + n, source(), dst, axis, step)

    def ring_start(self, phase):
        for n in range(4):
            self.ring_copy(phase, n).start()

    def ring_mid(self, phase):
        axis, at, src, one, two, k = self.ring(phase)
        self.ring_copy(phase, 0).wait_recv()
        _add_into(one.at[0], [one.at[0], src(at(1), 0)])
        self.ring_copy(phase, 4).start()
        self.ring_copy(phase, 1).wait_recv()
        _add_into(one.at[1], [one.at[1], src(at(-1), 1)])
        self.ring_copy(phase, 5).start()

    def ring_end(self, phase):
        for n in range(2, 6):
            self.ring_copy(phase, n).wait_recv()

    def y_part(self, side):
        m, r0, r, c0, c, order = self.spec
        return self.grads[m].at[:, :, side, pl.ds(r0, r), pl.ds(c0, c)]

    def y_copy(self):
        away = 1 - self.co[2]
        src = self.y_part(away) if self.y_first else self.H.at[:, :, away]
        return self.copy(6, src, self.b["b3"], "y", 0)

    def y_end(self):
        self.y_copy().wait_recv()
        if self.y_first:
            own = self.y_part(self.co[2])
            for i in range(4):
                _add_into(self.K.at[i], [own.at[i], self.K.at[i]])
            return
        for half in (0, 1):
            _add_into(
                self.K.at[half], [self.H.at[half, :, self.co[2]], self.b["b3"].at[half]]
            )

    def first_sum(self):
        self.ring_end(0)
        p = self.ring(0)[1](0)
        two = self.b["b2"]
        for half in (0, 1):
            _add_into(self.H.at[half], [self.g(p, half), two.at[0, half], two.at[1, half]])

    def last_sum(self):
        self.ring_end(1)
        p = self.ring(1)[1](0)
        two = self.b["c2"]
        m, r0, r, c0, c, order = self.spec
        h = c // 2
        for half in (0, 1):
            v = self.kk(p, half)[...].astype(f32) + two[0, half].astype(f32)
            v = v + two[1, half].astype(f32)
            if m == 3:
                self.outs[m][pl.ds(r0, r), c0 // HALF, pl.ds(c0 % HALF + half * h, h)] = v
            else:
                self.outs[m][pl.ds(r0, r), pl.ds(c0 + half * h, h)] = v

    def stage(self, n):
        if self.y_first:
            if n == 0:
                self.y_copy().start()
            elif n == 1:
                self.y_end()
                self.ring_start(0)
            elif n == 2:
                self.ring_mid(0)
            elif n == 3:
                self.first_sum()
                self.ring_start(1)
            elif n == 4:
                self.ring_mid(1)
            else:
                self.last_sum()
        elif n == 0:
            self.ring_start(0)
        elif n == 1:
            self.ring_mid(0)
        elif n == 2:
            self.first_sum()
            self.y_copy().start()
        elif n == 3:
            self.y_end()
            self.ring_start(1)
        elif n == 4:
            self.ring_mid(1)
        else:
            self.last_sum()

    def drain(self):
        for phase in (0, 1):
            for n in range(6):
                self.ring_copy(phase, n).wait_send()
        self.y_copy().wait_send()


def _nn(a, b):
    return lax.dot_general(a, b, (((1,), (0,)), ((), ())), preferred_element_type=f32)


def _nt(a, b):
    return lax.dot_general(a, b, (((1,), (1,)), ((), ())), preferred_element_type=f32)


def _tn(a, b):
    return lax.dot_general(a, b, (((0,), (0,)), ((), ())), preferred_element_type=f32)


def _norm(v):
    centre = v - jnp.mean(v, axis=-1, keepdims=True)
    inv = lax.rsqrt(jnp.mean(centre * centre, axis=-1, keepdims=True) + EPS)
    return centre * inv, inv


def _norm_back(upstream, hat, inv, gain):
    q = upstream * gain
    return inv * (
        q - jnp.mean(q, axis=-1, keepdims=True) - hat * jnp.mean(q * hat, axis=-1, keepdims=True)
    )


def _cols(i, n):
    return pl.ds(pl.multiple_of(i * n, n), n)


def _image_rows(img, body):
    base = img * PAD

    def step(i):
        for part in (0, 32):
            body(pl.ds(pl.multiple_of(base + i * 64 + part, 16), 32))

    _loop(3, step)
    body(pl.ds(base + 192, 16))


def _kernel(*refs):
    (counts, order, images, cotangent, gain_one, gain_two, wqkv_in, wo_in, w1_in, w2_in) = refs[:10]
    (y_ref, ig_ref, o_w2, o_w1, o_wo, o_qkv, o_gain) = refs[10:17]
    rest = refs[17:]
    (
        wqkv, wo, w1, w2, g_w2, g_w1, g_wo, g_qkv, g_gain,
        xb, eb, hin, n1, pr, pb, mx, mid, n2, act, gp, eg, mlow, pg, sendb, recvb, gacc,
        load_sem, x_ss, x_rs, hop_sem, rs_ss, rs_rs,
    ) = rest[:32]
    ring_bufs = rest[32:]

    section = lax.axis_index("section")
    tensor = lax.axis_index("tensor")
    dp = lax.axis_index("dp")
    z, x, y = dp // 8, lax.rem(dp // 2, 4), lax.rem(dp, 2)

    def load(i):
        if i < 3:
            src, dst = wqkv_in.at[i], wqkv.at[:, pl.ds(i * HALF, HALF)]
        else:
            src, dst = ((wo_in, wo), (w1_in, w1), (w2_in, w2))[i - 3]
        return pltpu.make_async_copy(src, dst, load_sem.at[i])

    for i in range(6):
        load(i).start()

    barrier = pltpu.get_barrier_semaphore()

    def r4(v):
        return lax.rem(v + 4, 4)

    for peer in (
        {"tensor": 1 - tensor},
        {"section": 1 - section},
        {"dp": r4(z + 1) * 8 + x * 2 + y},
        {"dp": r4(z - 1) * 8 + x * 2 + y},
        {"dp": z * 8 + r4(x + 1) * 2 + y},
        {"dp": z * 8 + r4(x - 1) * 2 + y},
        {"dp": z * 8 + x * 2 + 1 - y},
    ):
        pl.semaphore_signal(barrier, inc=1, device_id=peer, device_id_type=MESH)

    for img in range(IMGS):
        live = jnp.float32(0)
        for i in range(IMGS):
            held = jnp.where(jnp.logical_and(order[0, i] == img, i < counts[0]), 1.0, 0.0)
            live = live + held
        xb[pl.ds(img * PAD + TOKENS - 5, 16), :] = jnp.zeros((16, D), bf16)
        eb[pl.ds(img * PAD + TOKENS - 5, 16), :] = jnp.zeros((16, D), bf16)
        xb[pl.ds(img * PAD, TOKENS), :] = images[img]
        eb[pl.ds(img * PAD, TOKENS), :] = (cotangent[img].astype(f32) * live).astype(bf16)
    pl.semaphore_wait(barrier, 7)

    def img_rows(img):
        return pl.ds(img * PAD, PAD)

    def exchange(par, img):
        return pltpu.make_async_remote_copy(
            src_ref=sendb.at[par, img_rows(img)],
            dst_ref=recvb.at[par, img_rows(img)],
            send_sem=x_ss.at[par, img],
            recv_sem=x_rs.at[par, img],
            device_id={"tensor": 1 - tensor},
            device_id_type=MESH,
        )

    own_half = pl.ds(pl.multiple_of(tensor * 512, 512), 512)
    other_half = pl.ds(pl.multiple_of((1 - tensor) * 512, 512), 512)

    def hop(src, img):
        return pltpu.make_async_remote_copy(
            src_ref=src.at[img_rows(img), own_half],
            dst_ref=hin.at[img_rows(img), own_half],
            send_sem=hop_sem.at[0, img],
            recv_sem=hop_sem.at[1, img],
            device_id={"section": 1 - section},
            device_id_type=MESH,
        )

    def pass_half(img, cols):
        return pltpu.make_async_remote_copy(
            src_ref=hin.at[img_rows(img), cols],
            dst_ref=hin.at[img_rows(img), cols],
            send_sem=hop_sem.at[2, img],
            recv_sem=hop_sem.at[3, img],
            device_id={"tensor": 1 - tensor},
            device_id_type=MESH,
        )

    def receive(src, dst, img):
        hop(src, img).wait_recv()
        pass_half(img, own_half).start()
        pass_half(img, own_half).wait_send()
        pass_half(img, other_half).wait_recv()
        dst[img_rows(img), :] = hin[img_rows(img), :]

    lane = lax.broadcasted_iota(jnp.int32, (1, 128), 1)
    head_masks = ((lane < 64).astype(bf16), (lane >= 64).astype(bf16))
    key_bias = jnp.where(lax.broadcasted_iota(jnp.int32, (PAD, 1), 0) < TOKENS, 0.0, -1e30)

    def forward(tick):
        first = tick == 0

        @pl.when(jnp.logical_and(tick == 1, section == 0))
        def _():
            for img in (0, 1):
                hop(y_ref, img).wait_send()

        def ln_one(rows):
            hat, inv = _norm(xb[rows, :].astype(f32))
            n1[rows, :] = (hat * gain_one[...]).astype(bf16)

        def project(rows):
            def step(i):
                pr[rows, _cols(i, 512)] = _nn(n1[rows, :], wqkv[:, _cols(i, 512)]).astype(bf16)

            _loop(3, step)

        @pl.when(first)
        def _():
            _image_rows(0, ln_one)
            _image_rows(1, ln_one)
            for i in range(3):
                load(i).wait()
            project(pl.ds(0, ROWS))

        for img in (0, 1):
            @pl.when(tick == 1)
            def _():
                @pl.when(section == 1)
                def _():
                    receive(y_ref, xb, img)

                _image_rows(img, ln_one)
                project(img_rows(img))

            def attend(pair_i):
                rows = img_rows(img)
                q = pr[rows, _cols(pair_i, 128)]
                k = pr[rows, _cols(pair_i + 4, 128)]
                v = pr[rows, _cols(pair_i + 8, 128)]
                total = None
                for h in (0, 1):
                    s = _nt(k, q * (head_masks[h] * 0.125)) + key_bias
                    e = jnp.exp(s - jnp.max(s, axis=0, keepdims=True))
                    p = (e * (1.0 / jnp.sum(e, axis=0, keepdims=True))).astype(bf16)
                    pb[img * 8 + pair_i * 2 + h] = p
                    t = _tn(p, v * head_masks[h])
                    total = t if total is None else total + t
                mx[rows, _cols(pair_i, 128)] = total.astype(bf16)

            _loop(4, attend)

            if img == 0:
                @pl.when(first)
                def _():
                    load(3).wait()

            sendb[0, img_rows(img), :] = _nn(mx[img_rows(img), :], wo[...]).astype(bf16)
            exchange(0, img).start()

        for img in (0, 1):
            exchange(0, img).wait()

            def ln_two(rows):
                m = xb[rows, :].astype(f32) + (
                    sendb[0, rows, :].astype(f32) + recvb[0, rows, :].astype(f32)
                )
                mid[rows, :] = m
                hat, inv = _norm(m)
                n2[rows, :] = (hat * gain_two[...]).astype(bf16)

            _image_rows(img, ln_two)

        @pl.when(first)
        def _():
            load(4).wait()

        def expand(i):
            part = _cols(i, 256)
            e = _nn(n2[...], w1[:, part])
            phi = 0.5 * (1.0 + lax.erf(e * 0.7071067811865476))
            act[:, part] = (e * phi).astype(bf16)
            gp[:, part] = (phi + e * (jnp.exp(-0.5 * e * e) * 0.3989422804014327)).astype(bf16)

        _loop(8, expand)

        @pl.when(first)
        def _():
            load(5).wait()

        for img in (0, 1):
            def reduce(i):
                sendb[1, img_rows(img), _cols(i, 512)] = _nn(
                    act[img_rows(img), :], w2[:, _cols(i, 512)]
                ).astype(bf16)

            _loop(2, reduce)
            exchange(1, img).start()

        for img in (0, 1):
            exchange(1, img).wait()

            def finish(rows):
                v = mid[rows, :] + (sendb[1, rows, :].astype(f32) + recvb[1, rows, :].astype(f32))
                y_ref[rows, :] = v.astype(bf16)

            _image_rows(img, finish)

            @pl.when(jnp.logical_and(first, section == 0))
            def _():
                hop(y_ref, img).start()

    _loop(2, forward)

    grads = (g_w2, g_w1, g_wo, g_qkv, g_gain)
    outs = (o_w2, o_w1, o_wo, o_qkv, o_gain)
    nb = len(BUF_NAMES)
    streams = [
        _Stream(
            i, spec, grads, dict(zip(BUF_NAMES, ring_bufs[i * nb : (i + 1) * nb])), outs,
            (rs_ss, rs_rs), (z, x, y),
        )
        for i, spec in enumerate(STREAMS)
    ]
    groups, count = [], 0
    for g in GROUPS:
        groups.append(streams[count : count + len(g)])
        count += len(g)

    def steps(point):
        for i, stage in STEPS[point]:
            for st in groups[i]:
                st.stage(stage)

    def pack_gain(row, half):
        lanes = lax.broadcasted_iota(jnp.int32, (1024, 128), 0)
        pick = (lax.rem(lanes, 32) == lax.broadcasted_iota(jnp.int32, (1024, 128), 1)).astype(bf16)
        for zz in range(4):
            r = lax.broadcasted_iota(jnp.int32, (128, 1024), 0) // 16 + zz * 8
            c = lax.broadcasted_iota(jnp.int32, (128, 1024), 1) // 32
            spread = jnp.where(r == c, row, 0.0).astype(bf16)
            g_gain[zz, :, :, :, pl.ds(half * 128, 128)] = (
                _nn(spread, pick).astype(bf16).reshape(4, 2, 16, 128)
            )

    def backward(tick):
        last = tick == 1

        def expand_back(rows):
            def step(i):
                part = _cols(i, 256)
                d = _nt(eb[rows, :], w2[part, :])
                eg[rows, part] = (d * gp[rows, part].astype(f32)).astype(bf16)

            _loop(8, step)

        @pl.when(tick == 0)
        def _():
            expand_back(pl.ds(0, ROWS))

        @pl.when(jnp.logical_and(last, section == 1))
        def _():
            for img in (0, 1):
                hop(ig_ref, img).wait_send()

        @pl.when(jnp.logical_and(last, section == 0))
        def _():
            receive(ig_ref, eb, 0)

        @pl.when(last)
        def _():
            expand_back(img_rows(0))

        @pl.when(jnp.logical_and(last, section == 0))
        def _():
            receive(ig_ref, eb, 1)

        @pl.when(last)
        def _():
            def tile(i):
                for n in (0, 1):
                    part = pl.ds(n * 512, 512)
                    t = _tn(act[:, _cols(i, 256)], eb[:, part]).astype(bf16)
                    g_w2[i // 2, pl.ds(lax.rem(i, 2) * 2, 2), :, :, part] = t.reshape(2, 2, 64, 512)

            _loop(8, tile)
            steps("W2")
            expand_back(img_rows(1))
            steps("eb1")

        for img in (0, 1):
            def expand_terms(i):
                sendb[0, img_rows(img), _cols(i, 512)] = _nt(
                    eg[img_rows(img), :], w1[_cols(i, 512), :]
                ).astype(bf16)

            _loop(2, expand_terms)
            exchange(0, img).start()

        @pl.when(last)
        def _():
            def tile(i):
                for n in range(4):
                    part = pl.ds(n * 512, 512)
                    t = _tn(n2[:, _cols(i, 256)], eg[:, part]).astype(bf16)
                    g_w1[i, :, :, :, part] = t.reshape(4, 2, 32, 512)

            steps("et")
            _loop(4, tile)
            steps("W1")

        gacc[...] = jnp.zeros_like(gacc)

        for img in (0, 1):
            exchange(0, img).wait()

            def ln_two_back(rows):
                dn = sendb[0, rows, :].astype(f32) + recvb[0, rows, :].astype(f32)
                hat, inv = _norm(mid[rows, :])
                gacc[0:1, :] += jnp.sum(dn * hat, axis=0, keepdims=True)
                m = eb[rows, :].astype(f32) + _norm_back(dn, hat, inv, gain_two[...])
                mlow[rows, :] = m.astype(bf16)

            _image_rows(img, ln_two_back)

        sendb[1, :, pl.ds(0, HALF)] = _nt(mlow[...], wo[...]).astype(bf16)

        @pl.when(last)
        def _():
            steps("ln2")

            def tile(i):
                for n in (0, 1):
                    part = pl.ds(n * 512, 512)
                    t = _tn(mx[:, _cols(i, 256)], mlow[:, part]).astype(bf16)
                    g_wo[pl.ds(i * 2, 2), :, :, :, part] = t.reshape(2, 4, 2, 16, 512)

            _loop(2, tile)
            steps("Wo")

        def attend_back(img):
            def step(pair_i):
                rows = img_rows(img)
                q = pr[rows, _cols(pair_i, 128)]
                k = pr[rows, _cols(pair_i + 4, 128)]
                v = pr[rows, _cols(pair_i + 8, 128)]
                do = sendb[1, rows, _cols(pair_i, 128)]
                sums = [None, None, None]
                for h in (0, 1):
                    mask = head_masks[h]
                    p = pb[img * 8 + pair_i * 2 + h]
                    pf = p.astype(f32)
                    doh = do * mask
                    dpr = _nt(v, doh)
                    inner = jnp.sum(dpr * pf, axis=0, keepdims=True)
                    ds = (pf * (dpr - inner)).astype(bf16)
                    for j, t in enumerate((_tn(ds, k * mask), _nn(ds, q * mask), _nn(p, doh))):
                        sums[j] = t if sums[j] is None else sums[j] + t
                for j, scale in enumerate((0.125, 0.125, 1.0)):
                    pg[rows, _cols(pair_i + 4 * j, 128)] = (sums[j] * scale).astype(bf16)

            _loop(4, step)

        attend_back(0)

        @pl.when(last)
        def _():
            steps("at0")

        attend_back(1)

        @pl.when(last)
        def _():
            steps("at1")

        for img in (0, 1):
            def input_terms(i):
                sendb[1, img_rows(img), _cols(i, 512)] = _nt(
                    pg[img_rows(img), :], wqkv[_cols(i, 512), :]
                ).astype(bf16)

            _loop(2, input_terms)
            exchange(1, img).start()

        @pl.when(last)
        def _():
            def tile(i):
                for n in range(3):
                    part = pl.ds(n * 512, 512)
                    t = _tn(n1[:, _cols(i, 256)], pg[:, part]).astype(bf16)
                    g_qkv[i, :, :, :, part] = t.reshape(4, 2, 32, 512)

            steps("it")
            _loop(4, tile)
            steps("QKV")

        for img in (0, 1):
            exchange(1, img).wait()

            def ln_one_back(rows):
                dn = sendb[1, rows, :].astype(f32) + recvb[1, rows, :].astype(f32)
                hat, inv = _norm(xb[rows, :].astype(f32))
                gacc[1:2, :] += jnp.sum(dn * hat, axis=0, keepdims=True)
                m = mlow[rows, :].astype(f32) + _norm_back(dn, hat, inv, gain_one[...])
                ig_ref[rows, :] = m.astype(bf16)

            _image_rows(img, ln_one_back)

            @pl.when(jnp.logical_and(tick == 0, section == 1))
            def _():
                hop(ig_ref, img).start()

    _loop(2, backward)
    steps("ln1")
    pack_gain(gacc[1:2, :], 0)
    pack_gain(gacc[0:1, :], 1)
    steps("gain")
    steps("tail")
    for s in streams:
        s.drain()


def _call(*args):
    vmem = pl.BlockSpec(memory_space=pltpu.VMEM)
    hbm = pl.BlockSpec(memory_space=pl.ANY)
    smem = pl.BlockSpec(memory_space=pltpu.SMEM)
    out_shape = [jax.ShapeDtypeStruct((ROWS, D), bf16)] * 2 + [
        jax.ShapeDtypeStruct((32, 3, HALF) if s[1] == QKV else s, f32) for s in GRADS
    ]
    scratch = [
        pltpu.VMEM((D, QKV), bf16),
        pltpu.VMEM((HALF, D), bf16),
        pltpu.VMEM((D, WIDE), bf16),
        pltpu.VMEM((WIDE, D), bf16),
    ]
    scratch += [pltpu.VMEM((4, 4, 2) + s, bf16) for s in GRADS]
    scratch += [
        pltpu.VMEM((ROWS, D), bf16),
        pltpu.VMEM((ROWS, D), bf16),
        pltpu.VMEM((ROWS, D), bf16),
        pltpu.VMEM((ROWS, D), bf16),
        pltpu.VMEM((ROWS, QKV), bf16),
        pltpu.VMEM((16, PAD, PAD), bf16),
        pltpu.VMEM((ROWS, HALF), bf16),
        pltpu.VMEM((ROWS, D), f32),
        pltpu.VMEM((ROWS, D), bf16),
        pltpu.VMEM((ROWS, WIDE), bf16),
        pltpu.VMEM((ROWS, WIDE), bf16),
        pltpu.VMEM((ROWS, WIDE), bf16),
        pltpu.VMEM((ROWS, D), bf16),
        pltpu.VMEM((ROWS, QKV), bf16),
        pltpu.VMEM((2, ROWS, D), bf16),
        pltpu.VMEM((2, ROWS, D), bf16),
        pltpu.VMEM((8, D), f32),
        pltpu.SemaphoreType.DMA((6,)),
        pltpu.SemaphoreType.DMA((2, 2)),
        pltpu.SemaphoreType.DMA((2, 2)),
        pltpu.SemaphoreType.DMA((4, 2)),
        pltpu.SemaphoreType.DMA((len(STREAMS), 13)),
        pltpu.SemaphoreType.DMA((len(STREAMS), 13)),
    ]
    for s in STREAMS:
        scratch += [pltpu.VMEM(b, bf16) for b in _buffers(s)]
    return pl.pallas_call(
        _kernel,
        out_shape=out_shape,
        in_specs=[smem, smem, vmem, vmem, vmem, vmem, hbm, hbm, hbm, hbm],
        out_specs=[vmem] * len(out_shape),
        scratch_shapes=scratch,
        compiler_params=pltpu.CompilerParams(
            collective_id=0, has_side_effects=True, vmem_limit_bytes=63 << 20
        ),
    )(*args)


def per_device(
    images, cotangent, shard_count, slot_order, attend_gain, attend_input, attend_output,
    feed_gain, feed_expand, feed_reduce,
):
    y, ig, d_w2, d_w1, d_wo, d_qkv, d_gain = _call(
        shard_count, slot_order, images[0, :, 0], cotangent[0, :, 0], attend_gain, feed_gain,
        jnp.moveaxis(attend_input[0], 1, 0), attend_output[0], feed_expand[0], feed_reduce[0],
    )

    def cut(v):
        return v.reshape(IMGS, PAD, D)[:, :TOKENS].reshape(1, 1, IMGS, 1, TOKENS, D)

    return (
        cut(y), cut(ig), d_gain[0:1, 0:32], d_qkv[None], d_wo[None],
        d_gain[0:1, 128:160], d_w1[None], d_w2[None],
    )


def solution(mesh):
    in_specs = (
        P("dp", None, None, None, None),
        P("dp", None, None, None, None),
        P("dp"),
        P("dp", None),
        P("section", None),
        P("section", None, None, "tensor"),
        P("section", "tensor", None),
        P("section", None),
        P("section", None, "tensor"),
        P("section", "tensor", None),
    )
    out_specs = (
        P("section", "dp", None, None, None, None),
        P("section", "dp", None, None, None, None),
        P("section", "dp"),
        P("section", "dp", None, "tensor"),
        P("section", ("tensor", "dp"), None),
        P("section", "dp"),
        P("section", "dp", "tensor"),
        P("section", ("tensor", "dp"), None),
    )
    return jax.shard_map(
        per_device, mesh=mesh, in_specs=in_specs, out_specs=out_specs, check_vma=False
    )
```

```python
import functools

import jax
import jax.numpy as jnp
from jax import lax
from jax.experimental import pallas as pl
from jax.experimental.pallas import tpu as pltpu
from jax.sharding import PartitionSpec as P

f32 = jnp.float32
bf16 = jnp.bfloat16
MESH = pl.DeviceIdType.MESH

TOKENS = 197
PAD = 208
IMGS = 2
ROWS = IMGS * PAD
D = 1024
WIDE = 2048
HALF = 512
QKV = 3 * HALF
ROW_CHUNK = 32
N_CHUNK = ROWS // ROW_CHUNK
EPS = 1e-06

GRADS = ((64, D), (32, WIDE), (16, D), (32, QKV), (16, 256))


def _streams():
    groups = []

    def pair(m, r0, r, c0, c, order=0):
        groups.append(((m, r0, r, c0, c // 2, order), (m, r0, r, c0 + c // 2, c // 2, order + 1)))

    pair(0, 0, 64, 0, 512)
    pair(0, 0, 64, 512, 512, 2)
    pair(1, 0, 32, 0, 1024)
    pair(1, 0, 32, 1024, 1024)
    pair(2, 0, 16, 0, 1024)
    pair(3, 0, 32, 1024, 512)
    pair(3, 0, 32, 0, 512)
    pair(3, 0, 32, 512, 512)
    groups.append(((4, 0, 16, 0, 256, 0),))
    return groups


GROUPS = _streams()
STEPS = {
    "eb0": (),
    "W2": ((0, 0), (1, 0)),
    "eb1": (),
    "et": ((0, 1),),
    "W1": ((2, 0), (3, 0)),
    "ln2": ((0, 2),),
    "Wo": (),
    "at0": ((2, 1),),
    "at1": ((4, 0),),
    "it": ((3, 1),),
    "QKV": ((5, 0),),
    "ln1": ((6, 0), (1, 1), (2, 2)),
    "gain": ((4, 1),),
    "tail": ((0, 3), (3, 2), (5, 1), (7, 0), (6, 1), (2, 3), (1, 2), (8, 0), (4, 2), (0, 4), (3, 3), (5, 2), (7, 1), (4, 3), (6, 2), (2, 4), (5, 3), (1, 3), (8, 1), (0, 5), (3, 4), (6, 3), (7, 2), (4, 4), (2, 5), (5, 4), (1, 4), (8, 2), (3, 5), (6, 4), (4, 5), (5, 5), (1, 5), (7, 3), (6, 5), (8, 3), (7, 4), (8, 4), (7, 5), (8, 5)),
}
STREAMS = [s for g in GROUPS for s in g]
BUF_NAMES = ("b1", "b2", "b3", "c1", "c2")


def _buffers(spec):
    r, h = spec[2], spec[4] // 2
    if spec[5] >= 2:
        return ((2, 4, r, h), (2, 2, 4, r, h), (4, 4, r, 2 * h), (2, r, h), (2, 2, r, h))
    return (
        (2, 4, 2, r, h),
        (2, 2, 4, 2, r, h),
        (2, 4, r, h),
        (2, r, h),
        (2, 2, r, h),
    )


def _loop(n, body):
    def step(i, c):
        body(i)
        return c

    lax.fori_loop(0, n, step, 0)


def _add_into(dst, srcs):
    if len(dst.shape) == 2:
        v = srcs[0][...].astype(f32)
        for s in srcs[1:]:
            v = v + s[...].astype(f32)
        dst[...] = v.astype(dst.dtype)
        return

    def body(i):
        v = srcs[0][i].astype(f32)
        for s in srcs[1:]:
            v = v + s[i].astype(f32)
        dst[i] = v.astype(dst.dtype)

    _loop(dst.shape[0], body)


class _Stream:
    def __init__(self, index, spec, grads, bufs, outs, sems, coords):
        self.index, self.spec, self.grads, self.b, self.outs = index, spec, grads, bufs, outs
        self.send_sem, self.recv_sem = sems
        self.H = self.b["b2"].at[0]
        self.K = self.b["b3"]
        self.y_first = spec[5] >= 2
        self.co = coords

    def g(self, j, half):
        m, r0, r, c0, c, order = self.spec
        h = c // 2
        grad = self.grads[m]
        rows, cols = pl.ds(r0, r), pl.ds(c0 + half * h, h)
        if self.y_first:
            cols = pl.ds(half * h, h)
            return self.K.at[j, :, :, cols] if order == 2 else self.K.at[:, j, :, cols]
        return grad.at[j, :, :, rows, cols] if order == 0 else grad.at[:, j, :, rows, cols]

    def kk(self, j, half):
        return self.H.at[half, j] if self.y_first else self.K.at[half, j]

    def peer(self, axis, d):
        z, x, y = self.co
        if axis == "y":
            y = 1 - y
        elif axis == "z":
            z = lax.rem(z + d + 4, 4)
        else:
            x = lax.rem(x + d + 4, 4)
        return {"dp": z * 8 + x * 2 + y}

    def copy(self, k, src, dst, axis, d):
        return pltpu.make_async_remote_copy(
            src_ref=src,
            dst_ref=dst,
            send_sem=self.send_sem.at[self.index, k],
            recv_sem=self.recv_sem.at[self.index, k],
            device_id=self.peer(axis, d),
            device_id_type=MESH,
        )

    def ring(self, phase):
        axis = ("zx", "xz")[self.spec[5] % 2][phase]
        p = self.co[0] if axis == "z" else self.co[1]
        src = (self.g, self.kk)[phase]
        one, two = (self.b["b1"], self.b["b2"]) if phase == 0 else (self.b["c1"], self.b["c2"])
        return axis, (lambda d: lax.rem(p + d + 4, 4)), src, one, two, 7 * phase

    def ring_copy(self, phase, n):
        axis, at, src, one, two, k = self.ring(phase)
        source, dst, step = (
            (lambda: src(at(2), 0), one.at[0], 1),
            (lambda: src(at(2), 1), one.at[1], -1),
            (lambda: src(at(1), 1), two.at[0, 1], 1),
            (lambda: src(at(-1), 0), two.at[1, 0], -1),
            (lambda: one.at[0], two.at[0, 0], 1),
            (lambda: one.at[1], two.at[1, 1], -1),
        )[n]
        return self.copy(k + n, source(), dst, axis, step)

    def ring_start(self, phase):
        for n in range(4):
            self.ring_copy(phase, n).start()

    def ring_mid(self, phase):
        axis, at, src, one, two, k = self.ring(phase)
        self.ring_copy(phase, 0).wait_recv()
        _add_into(one.at[0], [one.at[0], src(at(1), 0)])
        self.ring_copy(phase, 4).start()
        self.ring_copy(phase, 1).wait_recv()
        _add_into(one.at[1], [one.at[1], src(at(-1), 1)])
        self.ring_copy(phase, 5).start()

    def ring_end(self, phase):
        for n in range(2, 6):
            self.ring_copy(phase, n).wait_recv()

    def y_part(self, side):
        m, r0, r, c0, c, order = self.spec
        return self.grads[m].at[:, :, side, pl.ds(r0, r), pl.ds(c0, c)]

    def y_copy(self):
        away = 1 - self.co[2]
        src = self.y_part(away) if self.y_first else self.H.at[:, :, away]
        return self.copy(6, src, self.b["b3"], "y", 0)

    def y_end(self):
        self.y_copy().wait_recv()
        if self.y_first:
            own = self.y_part(self.co[2])
            for i in range(4):
                _add_into(self.K.at[i], [own.at[i], self.K.at[i]])
            return
        for half in (0, 1):
            _add_into(
                self.K.at[half], [self.H.at[half, :, self.co[2]], self.b["b3"].at[half]]
            )

    def first_sum(self):
        self.ring_end(0)
        p = self.ring(0)[1](0)
        two = self.b["b2"]
        for half in (0, 1):
            _add_into(self.H.at[half], [self.g(p, half), two.at[0, half], two.at[1, half]])

    def last_sum(self):
        self.ring_end(1)
        p = self.ring(1)[1](0)
        two = self.b["c2"]
        m, r0, r, c0, c, order = self.spec
        h = c // 2
        for half in (0, 1):
            v = self.kk(p, half)[...].astype(f32) + two[0, half].astype(f32)
            v = v + two[1, half].astype(f32)
            if m == 3:
                self.outs[m][pl.ds(r0, r), c0 // HALF, pl.ds(c0 % HALF + half * h, h)] = v
            else:
                self.outs[m][pl.ds(r0, r), pl.ds(c0 + half * h, h)] = v

    def stage(self, n):
        if self.y_first:
            if n == 0:
                self.y_copy().start()
            elif n == 1:
                self.y_end()
                self.ring_start(0)
            elif n == 2:
                self.ring_mid(0)
            elif n == 3:
                self.first_sum()
                self.ring_start(1)
            elif n == 4:
                self.ring_mid(1)
            else:
                self.last_sum()
        elif n == 0:
            self.ring_start(0)
        elif n == 1:
            self.ring_mid(0)
        elif n == 2:
            self.first_sum()
            self.y_copy().start()
        elif n == 3:
            self.y_end()
            self.ring_start(1)
        elif n == 4:
            self.ring_mid(1)
        else:
            self.last_sum()

    def drain(self):
        for phase in (0, 1):
            for n in range(6):
                self.ring_copy(phase, n).wait_send()
        self.y_copy().wait_send()


def _nn(a, b):
    return lax.dot_general(a, b, (((1,), (0,)), ((), ())), preferred_element_type=f32)


def _nt(a, b):
    return lax.dot_general(a, b, (((1,), (1,)), ((), ())), preferred_element_type=f32)


def _tn(a, b):
    return lax.dot_general(a, b, (((0,), (0,)), ((), ())), preferred_element_type=f32)


def _norm(v):
    centre = v - jnp.mean(v, axis=-1, keepdims=True)
    inv = lax.rsqrt(jnp.mean(centre * centre, axis=-1, keepdims=True) + EPS)
    return centre * inv, inv


def _norm_back(upstream, hat, inv, gain):
    q = upstream * gain
    return inv * (
        q - jnp.mean(q, axis=-1, keepdims=True) - hat * jnp.mean(q * hat, axis=-1, keepdims=True)
    )


def _cols(i, n):
    return pl.ds(pl.multiple_of(i * n, n), n)


def _image_rows(img, body):
    base = img * PAD

    def step(i):
        for part in (0, 32):
            body(pl.ds(pl.multiple_of(base + i * 64 + part, 16), 32))

    _loop(3, step)
    body(pl.ds(base + 192, 16))


def _kernel(*refs):
    (counts, order, images, cotangent, gain_one, gain_two, wqkv_in, wo_in, w1_in, w2_in) = refs[:10]
    (y_ref, ig_ref, o_w2, o_w1, o_wo, o_qkv, o_gain) = refs[10:17]
    rest = refs[17:]
    (
        wqkv, wo, w1, w2, g_w2, g_w1, g_wo, g_qkv, g_gain,
        xb, eb, hin, n1, pr, pb, mx, mid, n2, act, gp, eg, mlow, pg, sendb, recvb, gacc,
        load_sem, x_ss, x_rs, hop_sem, rs_ss, rs_rs,
    ) = rest[:32]
    ring_bufs = rest[32:]

    section = lax.axis_index("section")
    tensor = lax.axis_index("tensor")
    dp = lax.axis_index("dp")
    z, x, y = dp // 8, lax.rem(dp // 2, 4), lax.rem(dp, 2)

    def load(i):
        if i < 3:
            src, dst = wqkv_in.at[i], wqkv.at[:, pl.ds(i * HALF, HALF)]
        else:
            src, dst = ((wo_in, wo), (w1_in, w1), (w2_in, w2))[i - 3]
        return pltpu.make_async_copy(src, dst, load_sem.at[i])

    for i in range(6):
        load(i).start()

    barrier = pltpu.get_barrier_semaphore()

    def r4(v):
        return lax.rem(v + 4, 4)

    for peer in (
        {"tensor": 1 - tensor},
        {"section": 1 - section},
        {"dp": r4(z + 1) * 8 + x * 2 + y},
        {"dp": r4(z - 1) * 8 + x * 2 + y},
        {"dp": z * 8 + r4(x + 1) * 2 + y},
        {"dp": z * 8 + r4(x - 1) * 2 + y},
        {"dp": z * 8 + x * 2 + 1 - y},
    ):
        pl.semaphore_signal(barrier, inc=1, device_id=peer, device_id_type=MESH)

    for img in range(IMGS):
        live = jnp.float32(0)
        for i in range(IMGS):
            held = jnp.where(jnp.logical_and(order[0, i] == img, i < counts[0]), 1.0, 0.0)
            live = live + held
        xb[pl.ds(img * PAD + TOKENS - 5, 16), :] = jnp.zeros((16, D), bf16)
        eb[pl.ds(img * PAD + TOKENS - 5, 16), :] = jnp.zeros((16, D), bf16)
        xb[pl.ds(img * PAD, TOKENS), :] = images[img]
        eb[pl.ds(img * PAD, TOKENS), :] = (cotangent[img].astype(f32) * live).astype(bf16)
    pl.semaphore_wait(barrier, 7)

    def img_rows(img):
        return pl.ds(img * PAD, PAD)

    def exchange(par, img):
        return pltpu.make_async_remote_copy(
            src_ref=sendb.at[par, img_rows(img)],
            dst_ref=recvb.at[par, img_rows(img)],
            send_sem=x_ss.at[par, img],
            recv_sem=x_rs.at[par, img],
            device_id={"tensor": 1 - tensor},
            device_id_type=MESH,
        )

    own_half = pl.ds(pl.multiple_of(tensor * 512, 512), 512)
    other_half = pl.ds(pl.multiple_of((1 - tensor) * 512, 512), 512)

    def hop(src, img):
        return pltpu.make_async_remote_copy(
            src_ref=src.at[img_rows(img), own_half],
            dst_ref=hin.at[img_rows(img), own_half],
            send_sem=hop_sem.at[0, img],
            recv_sem=hop_sem.at[1, img],
            device_id={"section": 1 - section},
            device_id_type=MESH,
        )

    def pass_half(img, cols):
        return pltpu.make_async_remote_copy(
            src_ref=hin.at[img_rows(img), cols],
            dst_ref=hin.at[img_rows(img), cols],
            send_sem=hop_sem.at[2, img],
            recv_sem=hop_sem.at[3, img],
            device_id={"tensor": 1 - tensor},
            device_id_type=MESH,
        )

    def receive(src, dst, img):
        hop(src, img).wait_recv()
        pass_half(img, own_half).start()
        pass_half(img, own_half).wait_send()
        pass_half(img, other_half).wait_recv()
        dst[img_rows(img), :] = hin[img_rows(img), :]

    lane = lax.broadcasted_iota(jnp.int32, (1, 128), 1)
    head_masks = ((lane < 64).astype(bf16), (lane >= 64).astype(bf16))
    key_bias = jnp.where(lax.broadcasted_iota(jnp.int32, (PAD, 1), 0) < TOKENS, 0.0, -1e30)

    def forward(tick):
        first = tick == 0

        @pl.when(jnp.logical_and(tick == 1, section == 0))
        def _():
            for img in (0, 1):
                hop(y_ref, img).wait_send()

        def ln_one(rows):
            hat, inv = _norm(xb[rows, :].astype(f32))
            n1[rows, :] = (hat * gain_one[...]).astype(bf16)

        def project(rows):
            def step(i):
                pr[rows, _cols(i, 512)] = _nn(n1[rows, :], wqkv[:, _cols(i, 512)]).astype(bf16)

            _loop(3, step)

        @pl.when(first)
        def _():
            _image_rows(0, ln_one)
            _image_rows(1, ln_one)
            for i in range(3):
                load(i).wait()
            project(pl.ds(0, ROWS))

        for img in (0, 1):
            @pl.when(tick == 1)
            def _():
                @pl.when(section == 1)
                def _():
                    receive(y_ref, xb, img)

                _image_rows(img, ln_one)
                project(img_rows(img))

            def attend(pair_i):
                rows = img_rows(img)
                q = pr[rows, _cols(pair_i, 128)]
                k = pr[rows, _cols(pair_i + 4, 128)]
                v = pr[rows, _cols(pair_i + 8, 128)]
                total = None
                for h in (0, 1):
                    s = _nt(k, q * (head_masks[h] * 0.125)) + key_bias
                    e = jnp.exp(s - jnp.max(s, axis=0, keepdims=True))
                    p = (e * (1.0 / jnp.sum(e, axis=0, keepdims=True))).astype(bf16)
                    pb[img * 8 + pair_i * 2 + h] = p
                    t = _tn(p, v * head_masks[h])
                    total = t if total is None else total + t
                mx[rows, _cols(pair_i, 128)] = total.astype(bf16)

            for pair_static in range(4):
                attend(pair_static)

            if img == 0:
                @pl.when(first)
                def _():
                    load(3).wait()

            sendb[0, img_rows(img), :] = _nn(mx[img_rows(img), :], wo[...]).astype(bf16)
            exchange(0, img).start()

        for img in (0, 1):
            exchange(0, img).wait()

            def ln_two(rows):
                m = xb[rows, :].astype(f32) + (
                    sendb[0, rows, :].astype(f32) + recvb[0, rows, :].astype(f32)
                )
                mid[rows, :] = m
                hat, inv = _norm(m)
                n2[rows, :] = (hat * gain_two[...]).astype(bf16)

            _image_rows(img, ln_two)

        @pl.when(first)
        def _():
            load(4).wait()

        def expand(i):
            part = _cols(i, 256)
            e = _nn(n2[...], w1[:, part])
            phi = 0.5 * (1.0 + lax.erf(e * 0.7071067811865476))
            act[:, part] = (e * phi).astype(bf16)
            gp[:, part] = (phi + e * (jnp.exp(-0.5 * e * e) * 0.3989422804014327)).astype(bf16)

        _loop(8, expand)

        @pl.when(first)
        def _():
            load(5).wait()

        for img in (0, 1):
            def reduce(i):
                sendb[1, img_rows(img), _cols(i, 512)] = _nn(
                    act[img_rows(img), :], w2[:, _cols(i, 512)]
                ).astype(bf16)

            _loop(2, reduce)
            exchange(1, img).start()

        for img in (0, 1):
            exchange(1, img).wait()

            def finish(rows):
                v = mid[rows, :] + (sendb[1, rows, :].astype(f32) + recvb[1, rows, :].astype(f32))
                y_ref[rows, :] = v.astype(bf16)

            _image_rows(img, finish)

            @pl.when(jnp.logical_and(first, section == 0))
            def _():
                hop(y_ref, img).start()

    _loop(2, forward)

    grads = (g_w2, g_w1, g_wo, g_qkv, g_gain)
    outs = (o_w2, o_w1, o_wo, o_qkv, o_gain)
    nb = len(BUF_NAMES)
    streams = [
        _Stream(
            i, spec, grads, dict(zip(BUF_NAMES, ring_bufs[i * nb : (i + 1) * nb])), outs,
            (rs_ss, rs_rs), (z, x, y),
        )
        for i, spec in enumerate(STREAMS)
    ]
    groups, count = [], 0
    for g in GROUPS:
        groups.append(streams[count : count + len(g)])
        count += len(g)

    def steps(point):
        for i, stage in STEPS[point]:
            for st in groups[i]:
                st.stage(stage)

    def pack_gain(row, half):
        lanes = lax.broadcasted_iota(jnp.int32, (1024, 128), 0)
        pick = (lax.rem(lanes, 32) == lax.broadcasted_iota(jnp.int32, (1024, 128), 1)).astype(bf16)
        for zz in range(4):
            r = lax.broadcasted_iota(jnp.int32, (128, 1024), 0) // 16 + zz * 8
            c = lax.broadcasted_iota(jnp.int32, (128, 1024), 1) // 32
            spread = jnp.where(r == c, row, 0.0).astype(bf16)
            g_gain[zz, :, :, :, pl.ds(half * 128, 128)] = (
                _nn(spread, pick).astype(bf16).reshape(4, 2, 16, 128)
            )

    def backward(tick):
        last = tick == 1

        def expand_back(rows):
            def step(i):
                part = _cols(i, 256)
                d = _nt(eb[rows, :], w2[part, :])
                eg[rows, part] = (d * gp[rows, part].astype(f32)).astype(bf16)

            _loop(8, step)

        @pl.when(tick == 0)
        def _():
            expand_back(pl.ds(0, ROWS))

        @pl.when(jnp.logical_and(last, section == 1))
        def _():
            for img in (0, 1):
                hop(ig_ref, img).wait_send()

        @pl.when(jnp.logical_and(last, section == 0))
        def _():
            receive(ig_ref, eb, 0)

        @pl.when(last)
        def _():
            expand_back(img_rows(0))

        @pl.when(jnp.logical_and(last, section == 0))
        def _():
            receive(ig_ref, eb, 1)

        @pl.when(last)
        def _():
            def tile(i):
                t = _tn(act[:, _cols(i, 256)], eb[...]).astype(bf16)
                g_w2[i // 2, pl.ds(lax.rem(i, 2) * 2, 2)] = t.reshape(2, 2, 64, D)

            _loop(8, tile)
            steps("W2")
            expand_back(img_rows(1))
            steps("eb1")

        for img in (0, 1):
            def expand_terms(i):
                sendb[0, img_rows(img), _cols(i, 512)] = _nt(
                    eg[img_rows(img), :], w1[_cols(i, 512), :]
                ).astype(bf16)

            _loop(2, expand_terms)
            exchange(0, img).start()

        @pl.when(last)
        def _():
            def tile(i):
                for n in (0, 1):
                    part = pl.ds(n * 1024, 1024)
                    t = _tn(n2[:, _cols(i, 256)], eg[:, part]).astype(bf16)
                    g_w1[i, :, :, :, part] = t.reshape(4, 2, 32, 1024)

            steps("et")
            _loop(4, tile)
            steps("W1")

        gacc[...] = jnp.zeros_like(gacc)

        for img in (0, 1):
            exchange(0, img).wait()

            def ln_two_back(rows):
                dn = sendb[0, rows, :].astype(f32) + recvb[0, rows, :].astype(f32)
                hat, inv = _norm(mid[rows, :])
                gacc[0:1, :] += jnp.sum(dn * hat, axis=0, keepdims=True)
                m = eb[rows, :].astype(f32) + _norm_back(dn, hat, inv, gain_two[...])
                mlow[rows, :] = m.astype(bf16)

            _image_rows(img, ln_two_back)

        sendb[1, :, pl.ds(0, HALF)] = _nt(mlow[...], wo[...]).astype(bf16)

        @pl.when(last)
        def _():
            steps("ln2")

            def tile(i):
                for n in (0, 1):
                    part = pl.ds(n * 512, 512)
                    t = _tn(mx[:, _cols(i, 256)], mlow[:, part]).astype(bf16)
                    g_wo[pl.ds(i * 2, 2), :, :, :, part] = t.reshape(2, 4, 2, 16, 512)

            _loop(2, tile)
            steps("Wo")

        def attend_back(img):
            def step(pair_i):
                rows = img_rows(img)
                q = pr[rows, _cols(pair_i, 128)]
                k = pr[rows, _cols(pair_i + 4, 128)]
                v = pr[rows, _cols(pair_i + 8, 128)]
                do = sendb[1, rows, _cols(pair_i, 128)]
                sums = [None, None, None]
                for h in (0, 1):
                    mask = head_masks[h]
                    p = pb[img * 8 + pair_i * 2 + h]
                    pf = p.astype(f32)
                    doh = do * mask
                    dpr = _nt(v, doh)
                    inner = jnp.sum(dpr * pf, axis=0, keepdims=True)
                    ds = (pf * (dpr - inner)).astype(bf16)
                    for j, t in enumerate((_tn(ds, k * mask), _nn(ds, q * mask), _nn(p, doh))):
                        sums[j] = t if sums[j] is None else sums[j] + t
                for j, scale in enumerate((0.125, 0.125, 1.0)):
                    pg[rows, _cols(pair_i + 4 * j, 128)] = (sums[j] * scale).astype(bf16)

            for pair_static in range(4):
                step(pair_static)

        attend_back(0)

        @pl.when(last)
        def _():
            steps("at0")

        attend_back(1)

        @pl.when(last)
        def _():
            steps("at1")

        for img in (0, 1):
            def input_terms(i):
                sendb[1, img_rows(img), _cols(i, 512)] = _nt(
                    pg[img_rows(img), :], wqkv[_cols(i, 512), :]
                ).astype(bf16)

            _loop(2, input_terms)
            exchange(1, img).start()

        @pl.when(last)
        def _():
            def tile(i):
                t = _tn(n1[:, _cols(i, 256)], pg[...]).astype(bf16)
                g_qkv[i] = t.reshape(4, 2, 32, QKV)

            steps("it")
            _loop(4, tile)
            steps("QKV")

        for img in (0, 1):
            exchange(1, img).wait()

            def ln_one_back(rows):
                dn = sendb[1, rows, :].astype(f32) + recvb[1, rows, :].astype(f32)
                hat, inv = _norm(xb[rows, :].astype(f32))
                gacc[1:2, :] += jnp.sum(dn * hat, axis=0, keepdims=True)
                m = mlow[rows, :].astype(f32) + _norm_back(dn, hat, inv, gain_one[...])
                ig_ref[rows, :] = m.astype(bf16)

            _image_rows(img, ln_one_back)

            @pl.when(jnp.logical_and(tick == 0, section == 1))
            def _():
                hop(ig_ref, img).start()

    _loop(2, backward)
    steps("ln1")
    pack_gain(gacc[1:2, :], 0)
    pack_gain(gacc[0:1, :], 1)
    steps("gain")
    steps("tail")
    for s in streams:
        s.drain()


def _call(*args):
    vmem = pl.BlockSpec(memory_space=pltpu.VMEM)
    hbm = pl.BlockSpec(memory_space=pl.ANY)
    smem = pl.BlockSpec(memory_space=pltpu.SMEM)
    out_shape = [jax.ShapeDtypeStruct((ROWS, D), bf16)] * 2 + [
        jax.ShapeDtypeStruct((32, 3, HALF) if s[1] == QKV else s, f32) for s in GRADS
    ]
    scratch = [
        pltpu.VMEM((D, QKV), bf16),
        pltpu.VMEM((HALF, D), bf16),
        pltpu.VMEM((D, WIDE), bf16),
        pltpu.VMEM((WIDE, D), bf16),
    ]
    scratch += [pltpu.VMEM((4, 4, 2) + s, bf16) for s in GRADS]
    scratch += [
        pltpu.VMEM((ROWS, D), bf16),
        pltpu.VMEM((ROWS, D), bf16),
        pltpu.VMEM((ROWS, D), bf16),
        pltpu.VMEM((ROWS, D), bf16),
        pltpu.VMEM((ROWS, QKV), bf16),
        pltpu.VMEM((16, PAD, PAD), bf16),
        pltpu.VMEM((ROWS, HALF), bf16),
        pltpu.VMEM((ROWS, D), f32),
        pltpu.VMEM((ROWS, D), bf16),
        pltpu.VMEM((ROWS, WIDE), bf16),
        pltpu.VMEM((ROWS, WIDE), bf16),
        pltpu.VMEM((ROWS, WIDE), bf16),
        pltpu.VMEM((ROWS, D), bf16),
        pltpu.VMEM((ROWS, QKV), bf16),
        pltpu.VMEM((2, ROWS, D), bf16),
        pltpu.VMEM((2, ROWS, D), bf16),
        pltpu.VMEM((8, D), f32),
        pltpu.SemaphoreType.DMA((6,)),
        pltpu.SemaphoreType.DMA((2, 2)),
        pltpu.SemaphoreType.DMA((2, 2)),
        pltpu.SemaphoreType.DMA((4, 2)),
        pltpu.SemaphoreType.DMA((len(STREAMS), 13)),
        pltpu.SemaphoreType.DMA((len(STREAMS), 13)),
    ]
    for s in STREAMS:
        scratch += [pltpu.VMEM(b, bf16) for b in _buffers(s)]
    return pl.pallas_call(
        _kernel,
        out_shape=out_shape,
        in_specs=[smem, smem, vmem, vmem, vmem, vmem, hbm, hbm, hbm, hbm],
        out_specs=[vmem] * len(out_shape),
        scratch_shapes=scratch,
        compiler_params=pltpu.CompilerParams(
            collective_id=0, has_side_effects=True, vmem_limit_bytes=63 << 20
        ),
    )(*args)


def per_device(
    images, cotangent, shard_count, slot_order, attend_gain, attend_input, attend_output,
    feed_gain, feed_expand, feed_reduce,
):
    y, ig, d_w2, d_w1, d_wo, d_qkv, d_gain = _call(
        shard_count, slot_order, images[0, :, 0], cotangent[0, :, 0], attend_gain, feed_gain,
        jnp.moveaxis(attend_input[0], 1, 0), attend_output[0], feed_expand[0], feed_reduce[0],
    )

    def cut(v):
        return v.reshape(IMGS, PAD, D)[:, :TOKENS].reshape(1, 1, IMGS, 1, TOKENS, D)

    return (
        cut(y), cut(ig), d_gain[0:1, 0:32], d_qkv[None], d_wo[None],
        d_gain[0:1, 128:160], d_w1[None], d_w2[None],
    )


def solution(mesh):
    in_specs = (
        P("dp", None, None, None, None),
        P("dp", None, None, None, None),
        P("dp"),
        P("dp", None),
        P("section", None),
        P("section", None, None, "tensor"),
        P("section", "tensor", None),
        P("section", None),
        P("section", None, "tensor"),
        P("section", "tensor", None),
    )
    out_specs = (
        P("section", "dp", None, None, None, None),
        P("section", "dp", None, None, None, None),
        P("section", "dp"),
        P("section", "dp", None, "tensor"),
        P("section", ("tensor", "dp"), None),
        P("section", "dp"),
        P("section", "dp", "tensor"),
        P("section", ("tensor", "dp"), None),
    )
    return jax.shard_map(
        per_device, mesh=mesh, in_specs=in_specs, out_specs=out_specs, check_vma=False
    )
```

```python
import functools

import jax
import jax.numpy as jnp
from jax import lax
from jax.experimental import pallas as pl
from jax.experimental.pallas import tpu as pltpu
from jax.sharding import PartitionSpec as P

f32 = jnp.float32
bf16 = jnp.bfloat16
MESH = pl.DeviceIdType.MESH

TOKENS = 197
PAD = 208
IMGS = 2
ROWS = IMGS * PAD
D = 1024
WIDE = 2048
HALF = 512
QKV = 3 * HALF
ROW_CHUNK = 32
N_CHUNK = ROWS // ROW_CHUNK
EPS = 1e-06

GRADS = ((64, D), (32, WIDE), (16, D), (32, QKV), (16, 256))


def _streams():
    groups = []

    def pair(m, r0, r, c0, c, order=0):
        groups.append(((m, r0, r, c0, c // 2, order), (m, r0, r, c0 + c // 2, c // 2, order + 1)))

    pair(0, 0, 64, 0, 512)
    pair(0, 0, 64, 512, 512, 2)
    pair(1, 0, 32, 0, 1024)
    pair(1, 0, 32, 1024, 1024)
    pair(2, 0, 16, 0, 1024)
    pair(3, 0, 32, 1024, 512)
    pair(3, 0, 32, 0, 512)
    pair(3, 0, 32, 512, 512)
    groups.append(((4, 0, 16, 0, 256, 0),))
    return groups


GROUPS = _streams()
STEPS = {
    "eb0": (),
    "W2": ((0, 0), (1, 0)),
    "eb1": (),
    "et": ((0, 1),),
    "W1": ((2, 0), (3, 0)),
    "ln2": ((0, 2),),
    "Wo": (),
    "at0": ((2, 1),),
    "at1": ((4, 0),),
    "it": ((3, 1),),
    "QKV": ((5, 0),),
    "ln1": ((6, 0), (1, 1), (2, 2)),
    "gain": ((4, 1),),
    "tail": ((0, 3), (3, 2), (5, 1), (7, 0), (6, 1), (2, 3), (1, 2), (8, 0), (4, 2), (0, 4), (3, 3), (5, 2), (7, 1), (4, 3), (6, 2), (2, 4), (5, 3), (1, 3), (8, 1), (0, 5), (3, 4), (6, 3), (7, 2), (4, 4), (2, 5), (5, 4), (1, 4), (8, 2), (3, 5), (6, 4), (4, 5), (5, 5), (1, 5), (7, 3), (6, 5), (8, 3), (7, 4), (8, 4), (7, 5), (8, 5)),
}
STREAMS = [s for g in GROUPS for s in g]
BUF_NAMES = ("b1", "b2", "b3", "c1", "c2")


def _buffers(spec):
    r, h = spec[2], spec[4] // 2
    if spec[5] >= 2:
        return ((2, 4, r, h), (2, 2, 4, r, h), (4, 4, r, 2 * h), (2, r, h), (2, 2, r, h))
    return (
        (2, 4, 2, r, h),
        (2, 2, 4, 2, r, h),
        (2, 4, r, h),
        (2, r, h),
        (2, 2, r, h),
    )


def _loop(n, body):
    def step(i, c):
        body(i)
        return c

    lax.fori_loop(0, n, step, 0)


def _loop2(n, body):
    def two(i):
        body(2 * i)
        body(2 * i + 1)

    _loop(n // 2, two)


def _add_into(dst, srcs):
    if len(dst.shape) == 2:
        v = srcs[0][...].astype(f32)
        for s in srcs[1:]:
            v = v + s[...].astype(f32)
        dst[...] = v.astype(dst.dtype)
        return

    def body(i):
        v = srcs[0][i].astype(f32)
        for s in srcs[1:]:
            v = v + s[i].astype(f32)
        dst[i] = v.astype(dst.dtype)

    _loop(dst.shape[0], body)


class _Stream:
    def __init__(self, index, spec, grads, bufs, outs, sems, coords):
        self.index, self.spec, self.grads, self.b, self.outs = index, spec, grads, bufs, outs
        self.send_sem, self.recv_sem = sems
        self.H = self.b["b2"].at[0]
        self.K = self.b["b3"]
        self.y_first = spec[5] >= 2
        self.co = coords

    def g(self, j, half):
        m, r0, r, c0, c, order = self.spec
        h = c // 2
        grad = self.grads[m]
        rows, cols = pl.ds(r0, r), pl.ds(c0 + half * h, h)
        if self.y_first:
            cols = pl.ds(half * h, h)
            return self.K.at[j, :, :, cols] if order == 2 else self.K.at[:, j, :, cols]
        return grad.at[j, :, :, rows, cols] if order == 0 else grad.at[:, j, :, rows, cols]

    def kk(self, j, half):
        return self.H.at[half, j] if self.y_first else self.K.at[half, j]

    def peer(self, axis, d):
        z, x, y = self.co
        if axis == "y":
            y = 1 - y
        elif axis == "z":
            z = lax.rem(z + d + 4, 4)
        else:
            x = lax.rem(x + d + 4, 4)
        return {"dp": z * 8 + x * 2 + y}

    def copy(self, k, src, dst, axis, d):
        return pltpu.make_async_remote_copy(
            src_ref=src,
            dst_ref=dst,
            send_sem=self.send_sem.at[self.index, k],
            recv_sem=self.recv_sem.at[self.index, k],
            device_id=self.peer(axis, d),
            device_id_type=MESH,
        )

    def ring(self, phase):
        axis = ("zx", "xz")[self.spec[5] % 2][phase]
        p = self.co[0] if axis == "z" else self.co[1]
        src = (self.g, self.kk)[phase]
        one, two = (self.b["b1"], self.b["b2"]) if phase == 0 else (self.b["c1"], self.b["c2"])
        return axis, (lambda d: lax.rem(p + d + 4, 4)), src, one, two, 7 * phase

    def ring_copy(self, phase, n):
        axis, at, src, one, two, k = self.ring(phase)
        source, dst, step = (
            (lambda: src(at(2), 0), one.at[0], 1),
            (lambda: src(at(2), 1), one.at[1], -1),
            (lambda: src(at(1), 1), two.at[0, 1], 1),
            (lambda: src(at(-1), 0), two.at[1, 0], -1),
            (lambda: one.at[0], two.at[0, 0], 1),
            (lambda: one.at[1], two.at[1, 1], -1),
        )[n]
        return self.copy(k + n, source(), dst, axis, step)

    def ring_start(self, phase):
        for n in range(4):
            self.ring_copy(phase, n).start()

    def ring_mid(self, phase):
        axis, at, src, one, two, k = self.ring(phase)
        self.ring_copy(phase, 0).wait_recv()
        _add_into(one.at[0], [one.at[0], src(at(1), 0)])
        self.ring_copy(phase, 4).start()
        self.ring_copy(phase, 1).wait_recv()
        _add_into(one.at[1], [one.at[1], src(at(-1), 1)])
        self.ring_copy(phase, 5).start()

    def ring_end(self, phase):
        for n in range(2, 6):
            self.ring_copy(phase, n).wait_recv()

    def y_part(self, side):
        m, r0, r, c0, c, order = self.spec
        return self.grads[m].at[:, :, side, pl.ds(r0, r), pl.ds(c0, c)]

    def y_copy(self):
        away = 1 - self.co[2]
        src = self.y_part(away) if self.y_first else self.H.at[:, :, away]
        return self.copy(6, src, self.b["b3"], "y", 0)

    def y_end(self):
        self.y_copy().wait_recv()
        if self.y_first:
            own = self.y_part(self.co[2])
            for i in range(4):
                _add_into(self.K.at[i], [own.at[i], self.K.at[i]])
            return
        for half in (0, 1):
            _add_into(
                self.K.at[half], [self.H.at[half, :, self.co[2]], self.b["b3"].at[half]]
            )

    def first_sum(self):
        self.ring_end(0)
        p = self.ring(0)[1](0)
        two = self.b["b2"]
        for half in (0, 1):
            _add_into(self.H.at[half], [self.g(p, half), two.at[0, half], two.at[1, half]])

    def last_sum(self):
        self.ring_end(1)
        p = self.ring(1)[1](0)
        two = self.b["c2"]
        m, r0, r, c0, c, order = self.spec
        h = c // 2
        for half in (0, 1):
            v = self.kk(p, half)[...].astype(f32) + two[0, half].astype(f32)
            v = v + two[1, half].astype(f32)
            if m == 3:
                self.outs[m][pl.ds(r0, r), c0 // HALF, pl.ds(c0 % HALF + half * h, h)] = v
            else:
                self.outs[m][pl.ds(r0, r), pl.ds(c0 + half * h, h)] = v

    def stage(self, n):
        if self.y_first:
            if n == 0:
                self.y_copy().start()
            elif n == 1:
                self.y_end()
                self.ring_start(0)
            elif n == 2:
                self.ring_mid(0)
            elif n == 3:
                self.first_sum()
                self.ring_start(1)
            elif n == 4:
                self.ring_mid(1)
            else:
                self.last_sum()
        elif n == 0:
            self.ring_start(0)
        elif n == 1:
            self.ring_mid(0)
        elif n == 2:
            self.first_sum()
            self.y_copy().start()
        elif n == 3:
            self.y_end()
            self.ring_start(1)
        elif n == 4:
            self.ring_mid(1)
        else:
            self.last_sum()

    def drain(self):
        for phase in (0, 1):
            for n in range(6):
                self.ring_copy(phase, n).wait_send()
        self.y_copy().wait_send()


def _nn(a, b):
    return lax.dot_general(a, b, (((1,), (0,)), ((), ())), preferred_element_type=f32)


def _nt(a, b):
    return lax.dot_general(a, b, (((1,), (1,)), ((), ())), preferred_element_type=f32)


def _tn(a, b):
    return lax.dot_general(a, b, (((0,), (0,)), ((), ())), preferred_element_type=f32)


def _norm(v):
    centre = v - jnp.mean(v, axis=-1, keepdims=True)
    inv = lax.rsqrt(jnp.mean(centre * centre, axis=-1, keepdims=True) + EPS)
    return centre * inv, inv


def _norm_back(upstream, hat, inv, gain):
    q = upstream * gain
    return inv * (
        q - jnp.mean(q, axis=-1, keepdims=True) - hat * jnp.mean(q * hat, axis=-1, keepdims=True)
    )


def _cols(i, n):
    return pl.ds(pl.multiple_of(i * n, n), n)


def _image_rows(img, body):
    base = img * PAD

    def step(i):
        for part in (0, 32):
            body(pl.ds(pl.multiple_of(base + i * 64 + part, 16), 32))

    _loop(3, step)
    body(pl.ds(base + 192, 16))


def _kernel(*refs):
    (counts, order, images, cotangent, gain_one, gain_two, wqkv_in, wo_in, w1_in, w2_in) = refs[:10]
    (y_ref, ig_ref, o_w2, o_w1, o_wo, o_qkv, o_gain) = refs[10:17]
    rest = refs[17:]
    (
        wqkv, wo, w1, w2, g_w2, g_w1, g_wo, g_qkv, g_gain,
        xb, eb, hin, n1, pr, pb, mx, mid, n2, act, gp, eg, mlow, pg, sendb, recvb, gacc,
        load_sem, x_ss, x_rs, hop_sem, rs_ss, rs_rs,
    ) = rest[:32]
    ring_bufs = rest[32:]

    section = lax.axis_index("section")
    tensor = lax.axis_index("tensor")
    dp = lax.axis_index("dp")
    z, x, y = dp // 8, lax.rem(dp // 2, 4), lax.rem(dp, 2)

    def load(i):
        if i < 3:
            src, dst = wqkv_in.at[i], wqkv.at[:, pl.ds(i * HALF, HALF)]
        else:
            src, dst = ((wo_in, wo), (w1_in, w1), (w2_in, w2))[i - 3]
        return pltpu.make_async_copy(src, dst, load_sem.at[i])

    for i in range(6):
        load(i).start()

    barrier = pltpu.get_barrier_semaphore()

    def r4(v):
        return lax.rem(v + 4, 4)

    for peer in (
        {"tensor": 1 - tensor},
        {"section": 1 - section},
        {"dp": r4(z + 1) * 8 + x * 2 + y},
        {"dp": r4(z - 1) * 8 + x * 2 + y},
        {"dp": z * 8 + r4(x + 1) * 2 + y},
        {"dp": z * 8 + r4(x - 1) * 2 + y},
        {"dp": z * 8 + x * 2 + 1 - y},
    ):
        pl.semaphore_signal(barrier, inc=1, device_id=peer, device_id_type=MESH)

    for img in range(IMGS):
        live = jnp.float32(0)
        for i in range(IMGS):
            held = jnp.where(jnp.logical_and(order[0, i] == img, i < counts[0]), 1.0, 0.0)
            live = live + held
        xb[pl.ds(img * PAD + TOKENS - 5, 16), :] = jnp.zeros((16, D), bf16)
        eb[pl.ds(img * PAD + TOKENS - 5, 16), :] = jnp.zeros((16, D), bf16)
        xb[pl.ds(img * PAD, TOKENS), :] = images[img]
        eb[pl.ds(img * PAD, TOKENS), :] = (cotangent[img].astype(f32) * live).astype(bf16)

    def img_rows(img):
        return pl.ds(img * PAD, PAD)

    def exchange(par, img):
        return pltpu.make_async_remote_copy(
            src_ref=sendb.at[par, img_rows(img)],
            dst_ref=recvb.at[par, img_rows(img)],
            send_sem=x_ss.at[par, img],
            recv_sem=x_rs.at[par, img],
            device_id={"tensor": 1 - tensor},
            device_id_type=MESH,
        )

    own_half = pl.ds(pl.multiple_of(tensor * 512, 512), 512)
    other_half = pl.ds(pl.multiple_of((1 - tensor) * 512, 512), 512)

    def hop(src, img):
        return pltpu.make_async_remote_copy(
            src_ref=src.at[img_rows(img), own_half],
            dst_ref=hin.at[img_rows(img), own_half],
            send_sem=hop_sem.at[0, img],
            recv_sem=hop_sem.at[1, img],
            device_id={"section": 1 - section},
            device_id_type=MESH,
        )

    def pass_half(img, cols):
        return pltpu.make_async_remote_copy(
            src_ref=hin.at[img_rows(img), cols],
            dst_ref=hin.at[img_rows(img), cols],
            send_sem=hop_sem.at[2, img],
            recv_sem=hop_sem.at[3, img],
            device_id={"tensor": 1 - tensor},
            device_id_type=MESH,
        )

    def receive(src, dst, img):
        hop(src, img).wait_recv()
        pass_half(img, own_half).start()
        pass_half(img, own_half).wait_send()
        pass_half(img, other_half).wait_recv()
        dst[img_rows(img), :] = hin[img_rows(img), :]

    lane = lax.broadcasted_iota(jnp.int32, (1, 128), 1)
    head_masks = ((lane < 64).astype(bf16), (lane >= 64).astype(bf16))
    key_bias = jnp.where(lax.broadcasted_iota(jnp.int32, (PAD, 1), 0) < TOKENS, 0.0, -1e30)

    def ln_one(rows):
        hat, inv = _norm(xb[rows, :].astype(f32))
        n1[rows, :] = (hat * gain_one[...]).astype(bf16)

    def project(rows):
        def step(i):
            pr[rows, _cols(i, 512)] = _nn(n1[rows, :], wqkv[:, _cols(i, 512)]).astype(bf16)

        _loop(3, step)

    _image_rows(0, ln_one)
    _image_rows(1, ln_one)
    for i in range(3):
        load(i).wait()
    project(pl.ds(0, ROWS))
    pl.semaphore_wait(barrier, 7)

    def forward(tick):
        first = tick == 0

        @pl.when(jnp.logical_and(tick == 1, section == 0))
        def _():
            for img in (0, 1):
                hop(y_ref, img).wait_send()

        for img in (0, 1):
            @pl.when(tick == 1)
            def _():
                @pl.when(section == 1)
                def _():
                    receive(y_ref, xb, img)

                _image_rows(img, ln_one)
                project(img_rows(img))

            def attend(pair_i):
                rows = img_rows(img)
                q = pr[rows, _cols(pair_i, 128)]
                k = pr[rows, _cols(pair_i + 4, 128)]
                v = pr[rows, _cols(pair_i + 8, 128)]
                total = None
                for h in (0, 1):
                    s = _nt(k, q * (head_masks[h] * 0.125)) + key_bias
                    e = jnp.exp(s - jnp.max(s, axis=0, keepdims=True))
                    p = (e * (1.0 / jnp.sum(e, axis=0, keepdims=True))).astype(bf16)
                    pb[img * 8 + pair_i * 2 + h] = p
                    t = _tn(p, v * head_masks[h])
                    total = t if total is None else total + t
                mx[rows, _cols(pair_i, 128)] = total.astype(bf16)

            for pair_static in range(4):
                attend(pair_static)

            if img == 0:
                @pl.when(first)
                def _():
                    load(3).wait()

            sendb[0, img_rows(img), :] = _nn(mx[img_rows(img), :], wo[...]).astype(bf16)
            exchange(0, img).start()

        for img in (0, 1):
            exchange(0, img).wait()

            def ln_two(rows):
                m = xb[rows, :].astype(f32) + (
                    sendb[0, rows, :].astype(f32) + recvb[0, rows, :].astype(f32)
                )
                mid[rows, :] = m
                hat, inv = _norm(m)
                n2[rows, :] = (hat * gain_two[...]).astype(bf16)

            _image_rows(img, ln_two)

        @pl.when(first)
        def _():
            load(4).wait()

        def expand(i):
            part = _cols(i, 256)
            e = _nn(n2[...], w1[:, part])
            phi = 0.5 * (1.0 + lax.erf(e * 0.7071067811865476))
            act[:, part] = (e * phi).astype(bf16)
            gp[:, part] = (phi + e * (jnp.exp(-0.5 * e * e) * 0.3989422804014327)).astype(bf16)

        _loop(8, expand)

        @pl.when(first)
        def _():
            load(5).wait()

        for img in (0, 1):
            def reduce(i):
                sendb[1, img_rows(img), _cols(i, 512)] = _nn(
                    act[img_rows(img), :], w2[:, _cols(i, 512)]
                ).astype(bf16)

            _loop(2, reduce)
            exchange(1, img).start()

        for img in (0, 1):
            exchange(1, img).wait()

            def finish(rows):
                v = mid[rows, :] + (sendb[1, rows, :].astype(f32) + recvb[1, rows, :].astype(f32))
                y_ref[rows, :] = v.astype(bf16)

            _image_rows(img, finish)

            @pl.when(jnp.logical_and(first, section == 0))
            def _():
                hop(y_ref, img).start()

    _loop(2, forward)

    grads = (g_w2, g_w1, g_wo, g_qkv, g_gain)
    outs = (o_w2, o_w1, o_wo, o_qkv, o_gain)
    nb = len(BUF_NAMES)
    streams = [
        _Stream(
            i, spec, grads, dict(zip(BUF_NAMES, ring_bufs[i * nb : (i + 1) * nb])), outs,
            (rs_ss, rs_rs), (z, x, y),
        )
        for i, spec in enumerate(STREAMS)
    ]
    groups, count = [], 0
    for g in GROUPS:
        groups.append(streams[count : count + len(g)])
        count += len(g)

    def steps(point):
        for i, stage in STEPS[point]:
            for st in groups[i]:
                st.stage(stage)

    def pack_gain(row, half):
        lanes = lax.broadcasted_iota(jnp.int32, (1024, 128), 0)
        pick = (lax.rem(lanes, 32) == lax.broadcasted_iota(jnp.int32, (1024, 128), 1)).astype(bf16)
        for zz in range(4):
            r = lax.broadcasted_iota(jnp.int32, (128, 1024), 0) // 16 + zz * 8
            c = lax.broadcasted_iota(jnp.int32, (128, 1024), 1) // 32
            spread = jnp.where(r == c, row, 0.0).astype(bf16)
            g_gain[zz, :, :, :, pl.ds(half * 128, 128)] = (
                _nn(spread, pick).astype(bf16).reshape(4, 2, 16, 128)
            )

    def backward(tick):
        last = tick == 1

        def expand_back(rows):
            def step(i):
                part = _cols(i, 256)
                d = _nt(eb[rows, :], w2[part, :])
                eg[rows, part] = (d * gp[rows, part].astype(f32)).astype(bf16)

            _loop2(8, step)

        @pl.when(tick == 0)
        def _():
            expand_back(pl.ds(0, ROWS))

        @pl.when(jnp.logical_and(last, section == 1))
        def _():
            for img in (0, 1):
                hop(ig_ref, img).wait_send()

        @pl.when(jnp.logical_and(last, section == 0))
        def _():
            receive(ig_ref, eb, 0)

        @pl.when(last)
        def _():
            expand_back(img_rows(0))

        @pl.when(jnp.logical_and(last, section == 0))
        def _():
            receive(ig_ref, eb, 1)

        @pl.when(last)
        def _():
            def tile(i):
                t = _tn(act[:, _cols(i, 256)], eb[...]).astype(bf16)
                g_w2[i // 2, pl.ds(lax.rem(i, 2) * 2, 2)] = t.reshape(2, 2, 64, D)

            _loop(8, tile)
            steps("W2")
            expand_back(img_rows(1))
            steps("eb1")

        for img in (0, 1):
            def expand_terms(i):
                sendb[0, img_rows(img), _cols(i, 512)] = _nt(
                    eg[img_rows(img), :], w1[_cols(i, 512), :]
                ).astype(bf16)

            _loop(2, expand_terms)
            exchange(0, img).start()

        @pl.when(last)
        def _():
            def tile(i):
                for n in (0, 1):
                    part = pl.ds(n * 1024, 1024)
                    t = _tn(n2[:, _cols(i, 256)], eg[:, part]).astype(bf16)
                    g_w1[i, :, :, :, part] = t.reshape(4, 2, 32, 1024)

            steps("et")
            _loop(4, tile)
            steps("W1")

        gacc[...] = jnp.zeros_like(gacc)

        for img in (0, 1):
            exchange(0, img).wait()

            def ln_two_back(rows):
                dn = sendb[0, rows, :].astype(f32) + recvb[0, rows, :].astype(f32)
                hat, inv = _norm(mid[rows, :])
                gacc[0:1, :] += jnp.sum(dn * hat, axis=0, keepdims=True)
                m = eb[rows, :].astype(f32) + _norm_back(dn, hat, inv, gain_two[...])
                mlow[rows, :] = m.astype(bf16)

            _image_rows(img, ln_two_back)

        sendb[1, :, pl.ds(0, HALF)] = _nt(mlow[...], wo[...]).astype(bf16)

        @pl.when(last)
        def _():
            steps("ln2")

            def tile(i):
                for n in (0, 1):
                    part = pl.ds(n * 512, 512)
                    t = _tn(mx[:, _cols(i, 256)], mlow[:, part]).astype(bf16)
                    g_wo[pl.ds(i * 2, 2), :, :, :, part] = t.reshape(2, 4, 2, 16, 512)

            _loop(2, tile)
            steps("Wo")

        def attend_back(img):
            def step(pair_i):
                rows = img_rows(img)
                q = pr[rows, _cols(pair_i, 128)]
                k = pr[rows, _cols(pair_i + 4, 128)]
                v = pr[rows, _cols(pair_i + 8, 128)]
                do = sendb[1, rows, _cols(pair_i, 128)]
                sums = [None, None, None]
                for h in (0, 1):
                    mask = head_masks[h]
                    p = pb[img * 8 + pair_i * 2 + h]
                    pf = p.astype(f32)
                    doh = do * mask
                    dpr = _nt(v, doh)
                    inner = jnp.sum(dpr * pf, axis=0, keepdims=True)
                    ds = (pf * (dpr - inner)).astype(bf16)
                    for j, t in enumerate((_tn(ds, k * mask), _nn(ds, q * mask), _nn(p, doh))):
                        sums[j] = t if sums[j] is None else sums[j] + t
                for j, scale in enumerate((0.125, 0.125, 1.0)):
                    pg[rows, _cols(pair_i + 4 * j, 128)] = (sums[j] * scale).astype(bf16)

            for pair_static in range(4):
                step(pair_static)

        attend_back(0)

        @pl.when(last)
        def _():
            steps("at0")

        attend_back(1)

        @pl.when(last)
        def _():
            steps("at1")

        for img in (0, 1):
            def input_terms(i):
                sendb[1, img_rows(img), _cols(i, 512)] = _nt(
                    pg[img_rows(img), :], wqkv[_cols(i, 512), :]
                ).astype(bf16)

            _loop(2, input_terms)
            exchange(1, img).start()

        @pl.when(last)
        def _():
            def tile(i):
                t = _tn(n1[:, _cols(i, 256)], pg[...]).astype(bf16)
                g_qkv[i] = t.reshape(4, 2, 32, QKV)

            steps("it")
            _loop(4, tile)
            steps("QKV")

        for img in (0, 1):
            exchange(1, img).wait()

            def ln_one_back(rows):
                dn = sendb[1, rows, :].astype(f32) + recvb[1, rows, :].astype(f32)
                hat, inv = _norm(xb[rows, :].astype(f32))
                gacc[1:2, :] += jnp.sum(dn * hat, axis=0, keepdims=True)
                m = mlow[rows, :].astype(f32) + _norm_back(dn, hat, inv, gain_one[...])
                ig_ref[rows, :] = m.astype(bf16)

            _image_rows(img, ln_one_back)

            @pl.when(jnp.logical_and(tick == 0, section == 1))
            def _():
                hop(ig_ref, img).start()

    _loop(2, backward)
    steps("ln1")
    pack_gain(gacc[1:2, :], 0)
    pack_gain(gacc[0:1, :], 1)
    steps("gain")
    steps("tail")
    for s in streams:
        s.drain()


def _call(*args):
    vmem = pl.BlockSpec(memory_space=pltpu.VMEM)
    hbm = pl.BlockSpec(memory_space=pl.ANY)
    smem = pl.BlockSpec(memory_space=pltpu.SMEM)
    out_shape = [jax.ShapeDtypeStruct((ROWS, D), bf16)] * 2 + [
        jax.ShapeDtypeStruct((32, 3, HALF) if s[1] == QKV else s, f32) for s in GRADS
    ]
    scratch = [
        pltpu.VMEM((D, QKV), bf16),
        pltpu.VMEM((HALF, D), bf16),
        pltpu.VMEM((D, WIDE), bf16),
        pltpu.VMEM((WIDE, D), bf16),
    ]
    scratch += [pltpu.VMEM((4, 4, 2) + s, bf16) for s in GRADS]
    scratch += [
        pltpu.VMEM((ROWS, D), bf16),
        pltpu.VMEM((ROWS, D), bf16),
        pltpu.VMEM((ROWS, D), bf16),
        pltpu.VMEM((ROWS, D), bf16),
        pltpu.VMEM((ROWS, QKV), bf16),
        pltpu.VMEM((16, PAD, PAD), bf16),
        pltpu.VMEM((ROWS, HALF), bf16),
        pltpu.VMEM((ROWS, D), f32),
        pltpu.VMEM((ROWS, D), bf16),
        pltpu.VMEM((ROWS, WIDE), bf16),
        pltpu.VMEM((ROWS, WIDE), bf16),
        pltpu.VMEM((ROWS, WIDE), bf16),
        pltpu.VMEM((ROWS, D), bf16),
        pltpu.VMEM((ROWS, QKV), bf16),
        pltpu.VMEM((2, ROWS, D), bf16),
        pltpu.VMEM((2, ROWS, D), bf16),
        pltpu.VMEM((8, D), f32),
        pltpu.SemaphoreType.DMA((6,)),
        pltpu.SemaphoreType.DMA((2, 2)),
        pltpu.SemaphoreType.DMA((2, 2)),
        pltpu.SemaphoreType.DMA((4, 2)),
        pltpu.SemaphoreType.DMA((len(STREAMS), 13)),
        pltpu.SemaphoreType.DMA((len(STREAMS), 13)),
    ]
    for s in STREAMS:
        scratch += [pltpu.VMEM(b, bf16) for b in _buffers(s)]
    return pl.pallas_call(
        _kernel,
        out_shape=out_shape,
        in_specs=[smem, smem, vmem, vmem, vmem, vmem, hbm, hbm, hbm, hbm],
        out_specs=[vmem] * len(out_shape),
        scratch_shapes=scratch,
        compiler_params=pltpu.CompilerParams(
            collective_id=0, has_side_effects=True, vmem_limit_bytes=63 << 20
        ),
    )(*args)


def per_device(
    images, cotangent, shard_count, slot_order, attend_gain, attend_input, attend_output,
    feed_gain, feed_expand, feed_reduce,
):
    y, ig, d_w2, d_w1, d_wo, d_qkv, d_gain = _call(
        shard_count, slot_order, images[0, :, 0], cotangent[0, :, 0], attend_gain, feed_gain,
        jnp.moveaxis(attend_input[0], 1, 0), attend_output[0], feed_expand[0], feed_reduce[0],
    )

    def cut(v):
        return v.reshape(IMGS, PAD, D)[:, :TOKENS].reshape(1, 1, IMGS, 1, TOKENS, D)

    return (
        cut(y), cut(ig), d_gain[0:1, 0:32], d_qkv[None], d_wo[None],
        d_gain[0:1, 128:160], d_w1[None], d_w2[None],
    )


def solution(mesh):
    in_specs = (
        P("dp", None, None, None, None),
        P("dp", None, None, None, None),
        P("dp"),
        P("dp", None),
        P("section", None),
        P("section", None, None, "tensor"),
        P("section", "tensor", None),
        P("section", None),
        P("section", None, "tensor"),
        P("section", "tensor", None),
    )
    out_specs = (
        P("section", "dp", None, None, None, None),
        P("section", "dp", None, None, None, None),
        P("section", "dp"),
        P("section", "dp", None, "tensor"),
        P("section", ("tensor", "dp"), None),
        P("section", "dp"),
        P("section", "dp", "tensor"),
        P("section", ("tensor", "dp"), None),
    )
    return jax.shard_map(
        per_device, mesh=mesh, in_specs=in_specs, out_specs=out_specs, check_vma=False
    )
```

```python
import functools

import jax
import jax.numpy as jnp
from jax import lax
from jax.experimental import pallas as pl
from jax.experimental.pallas import tpu as pltpu
from jax.sharding import PartitionSpec as P

f32 = jnp.float32
bf16 = jnp.bfloat16
MESH = pl.DeviceIdType.MESH

TOKENS = 197
PAD = 208
IMGS = 2
ROWS = IMGS * PAD
D = 1024
WIDE = 2048
HALF = 512
QKV = 3 * HALF
ROW_CHUNK = 32
N_CHUNK = ROWS // ROW_CHUNK
EPS = 1e-06

GRADS = ((64, D), (32, WIDE), (16, D), (32, QKV), (16, 256))


def _streams():
    groups = []

    def pair(m, r0, r, c0, c, order=0):
        groups.append(((m, r0, r, c0, c // 2, order), (m, r0, r, c0 + c // 2, c // 2, order + 1)))

    pair(0, 0, 64, 0, 512)
    pair(0, 0, 64, 512, 512, 2)
    pair(1, 0, 32, 0, 1024)
    pair(1, 0, 32, 1024, 1024)
    pair(2, 0, 16, 0, 1024)
    pair(3, 0, 32, 1024, 512)
    pair(3, 0, 32, 0, 512)
    pair(3, 0, 32, 512, 512)
    groups.append(((4, 0, 16, 0, 256, 0),))
    return groups


GROUPS = _streams()
STEPS = {
    "eb0": (),
    "W2": ((0, 0), (1, 0)),
    "eb1": (),
    "et": ((0, 1),),
    "W1": ((2, 0), (3, 0)),
    "ln2": ((0, 2),),
    "Wo": (),
    "at0": ((2, 1),),
    "at1": ((4, 0),),
    "it": ((3, 1),),
    "QKV": ((5, 0),),
    "ln1": ((6, 0), (1, 1), (2, 2)),
    "gain": ((4, 1),),
    "tail": ((0, 3), (3, 2), (5, 1), (7, 0), (6, 1), (2, 3), (1, 2), (8, 0), (4, 2), (0, 4), (3, 3), (5, 2), (7, 1), (4, 3), (6, 2), (2, 4), (5, 3), (1, 3), (8, 1), (0, 5), (3, 4), (6, 3), (7, 2), (4, 4), (2, 5), (5, 4), (1, 4), (8, 2), (3, 5), (6, 4), (4, 5), (5, 5), (1, 5), (7, 3), (6, 5), (8, 3), (7, 4), (8, 4), (7, 5), (8, 5)),
}
STREAMS = [s for g in GROUPS for s in g]
BUF_NAMES = ("b1", "b2", "b3", "c1", "c2")


def _buffers(spec):
    r, h = spec[2], spec[4] // 2
    if spec[5] >= 2:
        return ((2, 4, r, h), (2, 2, 4, r, h), (4, 4, r, 2 * h), (2, r, h), (2, 2, r, h))
    return (
        (2, 4, 2, r, h),
        (2, 2, 4, 2, r, h),
        (2, 4, r, h),
        (2, r, h),
        (2, 2, r, h),
    )


def _loop(n, body):
    def step(i, c):
        body(i)
        return c

    lax.fori_loop(0, n, step, 0)


def _loop2(n, body):
    def two(i):
        body(2 * i)
        body(2 * i + 1)

    _loop(n // 2, two)


def _add_into(dst, srcs):
    if len(dst.shape) == 2:
        v = srcs[0][...].astype(f32)
        for s in srcs[1:]:
            v = v + s[...].astype(f32)
        dst[...] = v.astype(dst.dtype)
        return

    def body(i):
        v = srcs[0][i].astype(f32)
        for s in srcs[1:]:
            v = v + s[i].astype(f32)
        dst[i] = v.astype(dst.dtype)

    _loop(dst.shape[0], body)


class _Stream:
    def __init__(self, index, spec, grads, bufs, outs, sems, coords):
        self.index, self.spec, self.grads, self.b, self.outs = index, spec, grads, bufs, outs
        self.send_sem, self.recv_sem = sems
        self.H = self.b["b2"].at[0]
        self.K = self.b["b3"]
        self.y_first = spec[5] >= 2
        self.co = coords

    def g(self, j, half):
        m, r0, r, c0, c, order = self.spec
        h = c // 2
        grad = self.grads[m]
        rows, cols = pl.ds(r0, r), pl.ds(c0 + half * h, h)
        if self.y_first:
            cols = pl.ds(half * h, h)
            return self.K.at[j, :, :, cols] if order == 2 else self.K.at[:, j, :, cols]
        return grad.at[j, :, :, rows, cols] if order == 0 else grad.at[:, j, :, rows, cols]

    def kk(self, j, half):
        return self.H.at[half, j] if self.y_first else self.K.at[half, j]

    def peer(self, axis, d):
        z, x, y = self.co
        if axis == "y":
            y = 1 - y
        elif axis == "z":
            z = lax.rem(z + d + 4, 4)
        else:
            x = lax.rem(x + d + 4, 4)
        return {"dp": z * 8 + x * 2 + y}

    def copy(self, k, src, dst, axis, d):
        return pltpu.make_async_remote_copy(
            src_ref=src,
            dst_ref=dst,
            send_sem=self.send_sem.at[self.index, k],
            recv_sem=self.recv_sem.at[self.index, k],
            device_id=self.peer(axis, d),
            device_id_type=MESH,
        )

    def ring(self, phase):
        axis = ("zx", "xz")[self.spec[5] % 2][phase]
        p = self.co[0] if axis == "z" else self.co[1]
        src = (self.g, self.kk)[phase]
        one, two = (self.b["b1"], self.b["b2"]) if phase == 0 else (self.b["c1"], self.b["c2"])
        return axis, (lambda d: lax.rem(p + d + 4, 4)), src, one, two, 7 * phase

    def ring_copy(self, phase, n):
        axis, at, src, one, two, k = self.ring(phase)
        source, dst, step = (
            (lambda: src(at(2), 0), one.at[0], 1),
            (lambda: src(at(2), 1), one.at[1], -1),
            (lambda: src(at(1), 1), two.at[0, 1], 1),
            (lambda: src(at(-1), 0), two.at[1, 0], -1),
            (lambda: one.at[0], two.at[0, 0], 1),
            (lambda: one.at[1], two.at[1, 1], -1),
        )[n]
        return self.copy(k + n, source(), dst, axis, step)

    def ring_start(self, phase):
        for n in range(4):
            self.ring_copy(phase, n).start()

    def ring_mid(self, phase):
        axis, at, src, one, two, k = self.ring(phase)
        self.ring_copy(phase, 0).wait_recv()
        _add_into(one.at[0], [one.at[0], src(at(1), 0)])
        self.ring_copy(phase, 4).start()
        self.ring_copy(phase, 1).wait_recv()
        _add_into(one.at[1], [one.at[1], src(at(-1), 1)])
        self.ring_copy(phase, 5).start()

    def ring_end(self, phase):
        for n in range(2, 6):
            self.ring_copy(phase, n).wait_recv()

    def y_part(self, side):
        m, r0, r, c0, c, order = self.spec
        return self.grads[m].at[:, :, side, pl.ds(r0, r), pl.ds(c0, c)]

    def y_copy(self):
        away = 1 - self.co[2]
        src = self.y_part(away) if self.y_first else self.H.at[:, :, away]
        return self.copy(6, src, self.b["b3"], "y", 0)

    def y_end(self):
        self.y_copy().wait_recv()
        if self.y_first:
            own = self.y_part(self.co[2])
            for i in range(4):
                _add_into(self.K.at[i], [own.at[i], self.K.at[i]])
            return
        for half in (0, 1):
            _add_into(
                self.K.at[half], [self.H.at[half, :, self.co[2]], self.b["b3"].at[half]]
            )

    def first_sum(self):
        self.ring_end(0)
        p = self.ring(0)[1](0)
        two = self.b["b2"]
        for half in (0, 1):
            _add_into(self.H.at[half], [self.g(p, half), two.at[0, half], two.at[1, half]])

    def last_sum(self):
        self.ring_end(1)
        p = self.ring(1)[1](0)
        two = self.b["c2"]
        m, r0, r, c0, c, order = self.spec
        h = c // 2
        for half in (0, 1):
            v = self.kk(p, half)[...].astype(f32) + two[0, half].astype(f32)
            v = v + two[1, half].astype(f32)
            if m == 3:
                self.outs[m][pl.ds(r0, r), c0 // HALF, pl.ds(c0 % HALF + half * h, h)] = v
            else:
                self.outs[m][pl.ds(r0, r), pl.ds(c0 + half * h, h)] = v

    def stage(self, n):
        if self.y_first:
            if n == 0:
                self.y_copy().start()
            elif n == 1:
                self.y_end()
                self.ring_start(0)
            elif n == 2:
                self.ring_mid(0)
            elif n == 3:
                self.first_sum()
                self.ring_start(1)
            elif n == 4:
                self.ring_mid(1)
            else:
                self.last_sum()
        elif n == 0:
            self.ring_start(0)
        elif n == 1:
            self.ring_mid(0)
        elif n == 2:
            self.first_sum()
            self.y_copy().start()
        elif n == 3:
            self.y_end()
            self.ring_start(1)
        elif n == 4:
            self.ring_mid(1)
        else:
            self.last_sum()

    def drain(self):
        for phase in (0, 1):
            for n in range(6):
                self.ring_copy(phase, n).wait_send()
        self.y_copy().wait_send()


def _nn(a, b):
    return lax.dot_general(a, b, (((1,), (0,)), ((), ())), preferred_element_type=f32)


def _nt(a, b):
    return lax.dot_general(a, b, (((1,), (1,)), ((), ())), preferred_element_type=f32)


def _tn(a, b):
    return lax.dot_general(a, b, (((0,), (0,)), ((), ())), preferred_element_type=f32)


def _norm(v):
    centre = v - jnp.mean(v, axis=-1, keepdims=True)
    inv = lax.rsqrt(jnp.mean(centre * centre, axis=-1, keepdims=True) + EPS)
    return centre * inv, inv


def _norm_back(upstream, hat, inv, gain):
    q = upstream * gain
    return inv * (
        q - jnp.mean(q, axis=-1, keepdims=True) - hat * jnp.mean(q * hat, axis=-1, keepdims=True)
    )


def _cols(i, n):
    return pl.ds(pl.multiple_of(i * n, n), n)


def _image_rows(img, body):
    base = img * PAD

    def step(i):
        for part in (0, 32):
            body(pl.ds(pl.multiple_of(base + i * 64 + part, 16), 32))

    _loop(3, step)
    body(pl.ds(base + 192, 16))


def _kernel(*refs):
    (counts, order, images, cotangent, gain_one, gain_two, wqkv_in, wo_in, w1_in, w2_in) = refs[:10]
    (y_ref, ig_ref, o_w2, o_w1, o_wo, o_qkv, o_gain) = refs[10:17]
    rest = refs[17:]
    (
        wqkv, wo, w1, w2, g_w2, g_w1, g_wo, g_qkv, g_gain,
        xb, eb, hin, n1, pr, pb, mx, mid, n2, act, gp, eg, mlow, pg, sendb, recvb, gacc,
        load_sem, x_ss, x_rs, hop_sem, rs_ss, rs_rs,
    ) = rest[:32]
    ring_bufs = rest[32:]

    section = lax.axis_index("section")
    tensor = lax.axis_index("tensor")
    dp = lax.axis_index("dp")
    z, x, y = dp // 8, lax.rem(dp // 2, 4), lax.rem(dp, 2)

    def load(i):
        if i < 3:
            src, dst = wqkv_in.at[i], wqkv.at[:, pl.ds(i * HALF, HALF)]
        else:
            src, dst = ((wo_in, wo), (w1_in, w1), (w2_in, w2))[i - 3]
        return pltpu.make_async_copy(src, dst, load_sem.at[i])

    for i in range(6):
        load(i).start()

    barrier = pltpu.get_barrier_semaphore()

    def r4(v):
        return lax.rem(v + 4, 4)

    for peer in (
        {"tensor": 1 - tensor},
        {"section": 1 - section},
        {"dp": r4(z + 1) * 8 + x * 2 + y},
        {"dp": r4(z - 1) * 8 + x * 2 + y},
        {"dp": z * 8 + r4(x + 1) * 2 + y},
        {"dp": z * 8 + r4(x - 1) * 2 + y},
        {"dp": z * 8 + x * 2 + 1 - y},
    ):
        pl.semaphore_signal(barrier, inc=1, device_id=peer, device_id_type=MESH)

    for img in range(IMGS):
        live = jnp.float32(0)
        for i in range(IMGS):
            held = jnp.where(jnp.logical_and(order[0, i] == img, i < counts[0]), 1.0, 0.0)
            live = live + held
        xb[pl.ds(img * PAD + TOKENS - 5, 16), :] = jnp.zeros((16, D), bf16)
        eb[pl.ds(img * PAD + TOKENS - 5, 16), :] = jnp.zeros((16, D), bf16)
        xb[pl.ds(img * PAD, TOKENS), :] = images[img]
        eb[pl.ds(img * PAD, TOKENS), :] = (cotangent[img].astype(f32) * live).astype(bf16)

    def img_rows(img):
        return pl.ds(img * PAD, PAD)

    def exchange(par, img):
        return pltpu.make_async_remote_copy(
            src_ref=sendb.at[par, img_rows(img)],
            dst_ref=recvb.at[par, img_rows(img)],
            send_sem=x_ss.at[par, img],
            recv_sem=x_rs.at[par, img],
            device_id={"tensor": 1 - tensor},
            device_id_type=MESH,
        )

    own_half = pl.ds(pl.multiple_of(tensor * 512, 512), 512)
    other_half = pl.ds(pl.multiple_of((1 - tensor) * 512, 512), 512)

    def hop(src, img):
        return pltpu.make_async_remote_copy(
            src_ref=src.at[img_rows(img), own_half],
            dst_ref=hin.at[img_rows(img), own_half],
            send_sem=hop_sem.at[0, img],
            recv_sem=hop_sem.at[1, img],
            device_id={"section": 1 - section},
            device_id_type=MESH,
        )

    def pass_half(img, cols):
        return pltpu.make_async_remote_copy(
            src_ref=hin.at[img_rows(img), cols],
            dst_ref=hin.at[img_rows(img), cols],
            send_sem=hop_sem.at[2, img],
            recv_sem=hop_sem.at[3, img],
            device_id={"tensor": 1 - tensor},
            device_id_type=MESH,
        )

    def receive(src, dst, img):
        hop(src, img).wait_recv()
        pass_half(img, own_half).start()
        pass_half(img, own_half).wait_send()
        pass_half(img, other_half).wait_recv()
        dst[img_rows(img), :] = hin[img_rows(img), :]

    lane = lax.broadcasted_iota(jnp.int32, (1, 128), 1)
    head_masks = ((lane < 64).astype(bf16), (lane >= 64).astype(bf16))
    key_bias = jnp.where(lax.broadcasted_iota(jnp.int32, (PAD, 1), 0) < TOKENS, 0.0, -1e30)

    def ln_one(rows):
        hat, inv = _norm(xb[rows, :].astype(f32))
        n1[rows, :] = (hat * gain_one[...]).astype(bf16)

    def project(rows):
        def step(i):
            pr[rows, _cols(i, 512)] = _nn(n1[rows, :], wqkv[:, _cols(i, 512)]).astype(bf16)

        _loop(3, step)

    _image_rows(0, ln_one)
    _image_rows(1, ln_one)
    for i in range(3):
        load(i).wait()
    project(pl.ds(0, ROWS))
    pl.semaphore_wait(barrier, 7)

    def forward(tick):
        first = tick == 0

        @pl.when(jnp.logical_and(tick == 1, section == 0))
        def _():
            for img in (0, 1):
                hop(y_ref, img).wait_send()

        for img in (0, 1):
            @pl.when(tick == 1)
            def _():
                @pl.when(section == 1)
                def _():
                    receive(y_ref, xb, img)

                _image_rows(img, ln_one)
                project(img_rows(img))

            def attend(pair_i):
                rows = img_rows(img)
                q = pr[rows, _cols(pair_i, 128)]
                k = pr[rows, _cols(pair_i + 4, 128)]
                v = pr[rows, _cols(pair_i + 8, 128)]
                total = None
                for h in (0, 1):
                    s = _nt(k, q * (head_masks[h] * 0.125)) + key_bias
                    e = jnp.exp(s - jnp.max(s, axis=0, keepdims=True))
                    p = (e * (1.0 / jnp.sum(e, axis=0, keepdims=True))).astype(bf16)
                    pb[img * 8 + pair_i * 2 + h] = p
                    t = _tn(p, v * head_masks[h])
                    total = t if total is None else total + t
                mx[rows, _cols(pair_i, 128)] = total.astype(bf16)

            for pair_static in range(4):
                attend(pair_static)

            if img == 0:
                @pl.when(first)
                def _():
                    load(3).wait()

            sendb[0, img_rows(img), :] = _nn(mx[img_rows(img), :], wo[...]).astype(bf16)
            exchange(0, img).start()

        for img in (0, 1):
            exchange(0, img).wait()

            def ln_two(rows):
                m = xb[rows, :].astype(f32) + (
                    sendb[0, rows, :].astype(f32) + recvb[0, rows, :].astype(f32)
                )
                mid[rows, :] = m
                hat, inv = _norm(m)
                n2[rows, :] = (hat * gain_two[...]).astype(bf16)

            _image_rows(img, ln_two)

        @pl.when(first)
        def _():
            load(4).wait()

        def expand(i):
            part = _cols(i, 256)
            e = _nn(n2[...], w1[:, part])
            phi = 0.5 * (1.0 + lax.erf(e * 0.7071067811865476))
            act[:, part] = (e * phi).astype(bf16)
            gp[:, part] = (phi + e * (jnp.exp(-0.5 * e * e) * 0.3989422804014327)).astype(bf16)

        _loop2(8, expand)

        @pl.when(first)
        def _():
            load(5).wait()

        for img in (0, 1):
            def reduce(i):
                sendb[1, img_rows(img), _cols(i, 512)] = _nn(
                    act[img_rows(img), :], w2[:, _cols(i, 512)]
                ).astype(bf16)

            _loop(2, reduce)
            exchange(1, img).start()

        for img in (0, 1):
            exchange(1, img).wait()

            def finish(rows):
                v = mid[rows, :] + (sendb[1, rows, :].astype(f32) + recvb[1, rows, :].astype(f32))
                y_ref[rows, :] = v.astype(bf16)

            _image_rows(img, finish)

            @pl.when(jnp.logical_and(first, section == 0))
            def _():
                hop(y_ref, img).start()

    _loop(2, forward)

    grads = (g_w2, g_w1, g_wo, g_qkv, g_gain)
    outs = (o_w2, o_w1, o_wo, o_qkv, o_gain)
    nb = len(BUF_NAMES)
    streams = [
        _Stream(
            i, spec, grads, dict(zip(BUF_NAMES, ring_bufs[i * nb : (i + 1) * nb])), outs,
            (rs_ss, rs_rs), (z, x, y),
        )
        for i, spec in enumerate(STREAMS)
    ]
    groups, count = [], 0
    for g in GROUPS:
        groups.append(streams[count : count + len(g)])
        count += len(g)

    def steps(point):
        for i, stage in STEPS[point]:
            for st in groups[i]:
                st.stage(stage)

    def pack_gain(row, half):
        lanes = lax.broadcasted_iota(jnp.int32, (1024, 128), 0)
        pick = (lax.rem(lanes, 32) == lax.broadcasted_iota(jnp.int32, (1024, 128), 1)).astype(bf16)
        for zz in range(4):
            r = lax.broadcasted_iota(jnp.int32, (128, 1024), 0) // 16 + zz * 8
            c = lax.broadcasted_iota(jnp.int32, (128, 1024), 1) // 32
            spread = jnp.where(r == c, row, 0.0).astype(bf16)
            g_gain[zz, :, :, :, pl.ds(half * 128, 128)] = (
                _nn(spread, pick).astype(bf16).reshape(4, 2, 16, 128)
            )

    def backward(tick):
        last = tick == 1

        def expand_back(rows):
            def step(i):
                part = _cols(i, 256)
                d = _nt(eb[rows, :], w2[part, :])
                eg[rows, part] = (d * gp[rows, part].astype(f32)).astype(bf16)

            _loop2(8, step)

        @pl.when(tick == 0)
        def _():
            expand_back(pl.ds(0, ROWS))

        @pl.when(jnp.logical_and(last, section == 1))
        def _():
            for img in (0, 1):
                hop(ig_ref, img).wait_send()

        @pl.when(jnp.logical_and(last, section == 0))
        def _():
            receive(ig_ref, eb, 0)

        @pl.when(last)
        def _():
            expand_back(img_rows(0))

        @pl.when(jnp.logical_and(last, section == 0))
        def _():
            receive(ig_ref, eb, 1)

        @pl.when(last)
        def _():
            def tile(i):
                t = _tn(act[:, _cols(i, 256)], eb[...]).astype(bf16)
                g_w2[i // 2, pl.ds(lax.rem(i, 2) * 2, 2)] = t.reshape(2, 2, 64, D)

            _loop(8, tile)
            steps("W2")
            expand_back(img_rows(1))
            steps("eb1")

        for img in (0, 1):
            def expand_terms(i):
                sendb[0, img_rows(img), _cols(i, 512)] = _nt(
                    eg[img_rows(img), :], w1[_cols(i, 512), :]
                ).astype(bf16)

            _loop(2, expand_terms)
            exchange(0, img).start()

        @pl.when(last)
        def _():
            def tile(i):
                for n in (0, 1):
                    part = pl.ds(n * 1024, 1024)
                    t = _tn(n2[:, _cols(i, 256)], eg[:, part]).astype(bf16)
                    g_w1[i, :, :, :, part] = t.reshape(4, 2, 32, 1024)

            steps("et")
            _loop(4, tile)
            steps("W1")

        gacc[...] = jnp.zeros_like(gacc)

        for img in (0, 1):
            exchange(0, img).wait()

            def ln_two_back(rows):
                dn = sendb[0, rows, :].astype(f32) + recvb[0, rows, :].astype(f32)
                hat, inv = _norm(mid[rows, :])
                gacc[0:1, :] += jnp.sum(dn * hat, axis=0, keepdims=True)
                m = eb[rows, :].astype(f32) + _norm_back(dn, hat, inv, gain_two[...])
                mlow[rows, :] = m.astype(bf16)

            _image_rows(img, ln_two_back)

        sendb[1, :, pl.ds(0, HALF)] = _nt(mlow[...], wo[...]).astype(bf16)

        @pl.when(last)
        def _():
            steps("ln2")

            def tile(i):
                for n in (0, 1):
                    part = pl.ds(n * 512, 512)
                    t = _tn(mx[:, _cols(i, 256)], mlow[:, part]).astype(bf16)
                    g_wo[pl.ds(i * 2, 2), :, :, :, part] = t.reshape(2, 4, 2, 16, 512)

            _loop(2, tile)
            steps("Wo")

        def attend_back(img):
            def step(pair_i):
                rows = img_rows(img)
                q = pr[rows, _cols(pair_i, 128)]
                k = pr[rows, _cols(pair_i + 4, 128)]
                v = pr[rows, _cols(pair_i + 8, 128)]
                do = sendb[1, rows, _cols(pair_i, 128)]
                sums = [None, None, None]
                for h in (0, 1):
                    mask = head_masks[h]
                    p = pb[img * 8 + pair_i * 2 + h]
                    pf = p.astype(f32)
                    doh = do * mask
                    dpr = _nt(v, doh)
                    inner = jnp.sum(dpr * pf, axis=0, keepdims=True)
                    ds = (pf * (dpr - inner)).astype(bf16)
                    for j, t in enumerate((_tn(ds, k * mask), _nn(ds, q * mask), _nn(p, doh))):
                        sums[j] = t if sums[j] is None else sums[j] + t
                for j, scale in enumerate((0.125, 0.125, 1.0)):
                    pg[rows, _cols(pair_i + 4 * j, 128)] = (sums[j] * scale).astype(bf16)

            for pair_static in range(4):
                step(pair_static)

        attend_back(0)

        @pl.when(last)
        def _():
            steps("at0")

        attend_back(1)

        @pl.when(last)
        def _():
            steps("at1")

        for img in (0, 1):
            def input_terms(i):
                sendb[1, img_rows(img), _cols(i, 512)] = _nt(
                    pg[img_rows(img), :], wqkv[_cols(i, 512), :]
                ).astype(bf16)

            _loop(2, input_terms)
            exchange(1, img).start()

        @pl.when(last)
        def _():
            def tile(i):
                t = _tn(n1[:, _cols(i, 256)], pg[...]).astype(bf16)
                g_qkv[i] = t.reshape(4, 2, 32, QKV)

            steps("it")
            _loop(4, tile)
            steps("QKV")

        for img in (0, 1):
            exchange(1, img).wait()

            def ln_one_back(rows):
                dn = sendb[1, rows, :].astype(f32) + recvb[1, rows, :].astype(f32)
                hat, inv = _norm(xb[rows, :].astype(f32))
                gacc[1:2, :] += jnp.sum(dn * hat, axis=0, keepdims=True)
                m = mlow[rows, :].astype(f32) + _norm_back(dn, hat, inv, gain_one[...])
                ig_ref[rows, :] = m.astype(bf16)

            _image_rows(img, ln_one_back)

            @pl.when(jnp.logical_and(tick == 0, section == 1))
            def _():
                hop(ig_ref, img).start()

    _loop(2, backward)
    steps("ln1")
    pack_gain(gacc[1:2, :], 0)
    pack_gain(gacc[0:1, :], 1)
    steps("gain")
    steps("tail")
    for s in streams:
        s.drain()


def _call(*args):
    vmem = pl.BlockSpec(memory_space=pltpu.VMEM)
    hbm = pl.BlockSpec(memory_space=pl.ANY)
    smem = pl.BlockSpec(memory_space=pltpu.SMEM)
    out_shape = [jax.ShapeDtypeStruct((ROWS, D), bf16)] * 2 + [
        jax.ShapeDtypeStruct((32, 3, HALF) if s[1] == QKV else s, f32) for s in GRADS
    ]
    scratch = [
        pltpu.VMEM((D, QKV), bf16),
        pltpu.VMEM((HALF, D), bf16),
        pltpu.VMEM((D, WIDE), bf16),
        pltpu.VMEM((WIDE, D), bf16),
    ]
    scratch += [pltpu.VMEM((4, 4, 2) + s, bf16) for s in GRADS]
    scratch += [
        pltpu.VMEM((ROWS, D), bf16),
        pltpu.VMEM((ROWS, D), bf16),
        pltpu.VMEM((ROWS, D), bf16),
        pltpu.VMEM((ROWS, D), bf16),
        pltpu.VMEM((ROWS, QKV), bf16),
        pltpu.VMEM((16, PAD, PAD), bf16),
        pltpu.VMEM((ROWS, HALF), bf16),
        pltpu.VMEM((ROWS, D), f32),
        pltpu.VMEM((ROWS, D), bf16),
        pltpu.VMEM((ROWS, WIDE), bf16),
        pltpu.VMEM((ROWS, WIDE), bf16),
        pltpu.VMEM((ROWS, WIDE), bf16),
        pltpu.VMEM((ROWS, D), bf16),
        pltpu.VMEM((ROWS, QKV), bf16),
        pltpu.VMEM((2, ROWS, D), bf16),
        pltpu.VMEM((2, ROWS, D), bf16),
        pltpu.VMEM((8, D), f32),
        pltpu.SemaphoreType.DMA((6,)),
        pltpu.SemaphoreType.DMA((2, 2)),
        pltpu.SemaphoreType.DMA((2, 2)),
        pltpu.SemaphoreType.DMA((4, 2)),
        pltpu.SemaphoreType.DMA((len(STREAMS), 13)),
        pltpu.SemaphoreType.DMA((len(STREAMS), 13)),
    ]
    for s in STREAMS:
        scratch += [pltpu.VMEM(b, bf16) for b in _buffers(s)]
    return pl.pallas_call(
        _kernel,
        out_shape=out_shape,
        in_specs=[smem, smem, vmem, vmem, vmem, vmem, hbm, hbm, hbm, hbm],
        out_specs=[vmem] * len(out_shape),
        scratch_shapes=scratch,
        compiler_params=pltpu.CompilerParams(
            collective_id=0, has_side_effects=True, vmem_limit_bytes=63 << 20
        ),
    )(*args)


def per_device(
    images, cotangent, shard_count, slot_order, attend_gain, attend_input, attend_output,
    feed_gain, feed_expand, feed_reduce,
):
    y, ig, d_w2, d_w1, d_wo, d_qkv, d_gain = _call(
        shard_count, slot_order, images[0, :, 0], cotangent[0, :, 0], attend_gain, feed_gain,
        jnp.moveaxis(attend_input[0], 1, 0), attend_output[0], feed_expand[0], feed_reduce[0],
    )

    def cut(v):
        return v.reshape(IMGS, PAD, D)[:, :TOKENS].reshape(1, 1, IMGS, 1, TOKENS, D)

    return (
        cut(y), cut(ig), d_gain[0:1, 0:32], d_qkv[None], d_wo[None],
        d_gain[0:1, 128:160], d_w1[None], d_w2[None],
    )


def solution(mesh):
    in_specs = (
        P("dp", None, None, None, None),
        P("dp", None, None, None, None),
        P("dp"),
        P("dp", None),
        P("section", None),
        P("section", None, None, "tensor"),
        P("section", "tensor", None),
        P("section", None),
        P("section", None, "tensor"),
        P("section", "tensor", None),
    )
    out_specs = (
        P("section", "dp", None, None, None, None),
        P("section", "dp", None, None, None, None),
        P("section", "dp"),
        P("section", "dp", None, "tensor"),
        P("section", ("tensor", "dp"), None),
        P("section", "dp"),
        P("section", "dp", "tensor"),
        P("section", ("tensor", "dp"), None),
    )
    return jax.shard_map(
        per_device, mesh=mesh, in_specs=in_specs, out_specs=out_specs, check_vma=False
    )
```
